128 devices in a mesh: section: 4 (over x), seq: 8 (over y_lo, z), mp: 4 (over y_hi, core).
Axes of the slice: x: 4, y: 4 (y_hi: 2, y_lo: 2; y = y_hi * 2 + y_lo), z: 4, core: 2. Of those that a mesh axis runs over, the one named last changes fastest.
Arguments:
- decoder_rows: bfloat16 [4, 4096, 4096], P('section', ('seq', 'mp'))
- encoder_panel: bfloat16 [4, 4096, 4096], P(None, 'seq', ('section', 'mp'))
- norm_gain: bfloat16 [4, 4096], P('section'), may hold values from 0.099609375 to 1.8984375
- w_query: bfloat16 [4, 4096, 2048], P('section', None, 'mp'), may hold values from -0.09375 to 0.09375
- w_key: bfloat16 [4, 4096, 2048], P('section', None, 'mp'), may hold values from -0.09375 to 0.09375
- w_value: bfloat16 [4, 4096, 2048], P('section', None, 'mp'), may hold values from -0.09375 to 0.09375
- w_output: bfloat16 [4, 2048, 4096], P('section', 'mp'), may hold values from -0.125 to 0.125
- decoder_segments: int32 [4, 4096], P('section', 'seq'), may hold values from 0 to 7, never falling along the last dimension, each value on 1 to 2048 neighbouring positions
- encoder_segments: int32 [4, 4096], P('section'), may hold values from 0 to 7, never falling along the last dimension, each value on 1 to 2048 neighbouring positions
Outputs:
- combined: bfloat16 [4, 4096, 4096], P('section', ('seq', 'mp'))
The draws below stay inside these ranges and needn't reach their ends.
Inputs may be any that keep to these rules, and one draw needn't show every extreme that they name: `decoder_segments`: ids never fall along a sequence; every one of the 8 documents has one or more decoder tokens in each micro-batch, and the longest one holds half of the decoder tokens. `encoder_segments`: ids never fall along a sequence; every one of the 8 documents has one or more encoder tokens in each micro-batch, and the longest one holds half of them.
All inputs are finite; a program needn't handle non-finite values.
Results may differ from the reference program's by a relative error of at most 0.017.
The reference program's roundings to bfloat16 on the way count: a program that leaves them out, or rounds other values in their place, can miss the bound.
Values may be sent and summed in bfloat16 or wider, within the bound.
No kernel may reach another device: no remote copies, remote signals or barrier semaphores. Data moves between devices by JAX's collectives and lax.ppermute only.
A program may use at most 128 MiB of HBM per device.

```python
import math
import jax
import jax.numpy as jnp
import numpy as np
from jax import lax

D = 4096
HD = 256
HEADS = 8
DOCS = 8
SECTIONS = 4
TOK = 4096
TE = 4096
HC = 2048


def draw_decoder_rows(key, part):
    key = jax.random.fold_in(key, 17)
    entry_key, row_key, column_key = jax.random.split(key, 3)
    entries = jax.random.normal(entry_key, (SECTIONS, TOK, D), jnp.float32)
    row_scale = jnp.exp(jax.random.uniform(row_key, (SECTIONS, TOK, 1), jnp.float32, math.log(0.2), math.log(2.0)))
    column_scale = jnp.exp(jax.random.uniform(column_key, (SECTIONS, 1, D), jnp.float32, math.log(0.3), math.log(3.0)))
    return (entries * row_scale * column_scale).astype(jnp.bfloat16)


def draw_encoder_panel(key, part):
    key = jax.random.fold_in(key, 29)
    entry_key, row_key = jax.random.split(key, 2)
    entries = jax.random.normal(entry_key, (SECTIONS, TE, D), jnp.float32)
    row_scale = jnp.exp(jax.random.uniform(row_key, (SECTIONS, TE, 1), jnp.float32, math.log(0.5), math.log(2.0)))
    return (entries * row_scale).astype(jnp.bfloat16)


def steps_of(stream_key, dims, cuts, smallest, top_value):
    factor_of = 1.0
    for position, shards_of in cuts:
        draws = jax.random.uniform(jax.random.fold_in(jax.random.fold_in(stream_key, 6), position), (shards_of,), jnp.float32, smallest / len(cuts), top_value / len(cuts))
        factor_of = factor_of * jnp.repeat(jnp.exp(draws), dims[position] // shards_of).reshape((-1,) + (1,) * (len(dims) - 1 - position))
    return factor_of


def length_profile(amount, total, reach, slope):
    portions = [(1 << 20) // math.isqrt(standing ** slope) + 1 for standing in range(2, amount + 1)]
    surplus, counts = total - reach - (amount - 1), [1] * (amount - 1)
    while surplus > 0:
        candidates = [i for i in range(amount - 1) if counts[i] < reach]
        pool, budget = sum([portions[i] for i in candidates]), surplus
        for i in candidates:
            addition = min(reach - counts[i], max(1, budget * portions[i] // pool), surplus)
            counts[i] = counts[i] + addition
            surplus = surplus - addition
    return np.array([reach] + counts)


def ragged(own_key, count, total, reach, slope):
    if count == 2:
        one = jax.random.randint(own_key, (), max(1, total - reach), min(reach, total - 1) + 1)
        return jnp.stack([one, total - one])
    sizes = jnp.asarray(length_profile(count, total, reach, slope), jnp.int32)
    twos = (count - 1) // 2
    giver, sink = sizes[1:1 + 2 * twos:2], sizes[2:2 + 2 * twos:2]
    room = jnp.minimum(giver - 1, reach - sink)
    shifted = jax.random.randint(jax.random.fold_in(own_key, 1), (twos,), 0, 1 << 20) % (room + 1)
    sizes = sizes.at[1:1 + 2 * twos:2].set(giver - shifted).at[2:2 + 2 * twos:2].set(sink + shifted)
    return sizes[jax.random.permutation(jax.random.fold_in(own_key, 2), count)]


def noise(stream_key, extent, scale, reach, cuts=(), kind=jnp.bfloat16):
    result = scale * jax.random.normal(stream_key, extent, jnp.float32)
    if cuts:
        result = result * steps_of(stream_key, extent, cuts, -0.22, 0.18)
    return jnp.clip(result, -reach, reach).astype(kind)


def setup_inputs(seed: int = 0) -> dict:
    splits = jax.random.split(jax.random.key(seed), 10)
    decoder_rows = draw_decoder_rows(jax.random.fold_in(splits[9], 71), 0)
    encoder_panel = draw_encoder_panel(jax.random.fold_in(splits[9], 71), 0)
    norm_gain = jnp.clip(1.0 + 0.18 * jax.random.normal(splits[2], (SECTIONS, D), jnp.float32), 0.099609375, 1.8984375).astype(jnp.bfloat16)
    w_query = noise(splits[3], (SECTIONS, D, HC), D ** -0.5, 0.09375, ((0, 4), (2, 4)))
    w_key = noise(splits[4], (SECTIONS, D, HC), D ** -0.5, 0.09375, ((0, 4), (2, 4)))
    w_value = noise(splits[5], (SECTIONS, D, HC), D ** -0.5, 0.09375, ((0, 4), (2, 4)))
    w_output = noise(splits[6], (SECTIONS, HC, D), HC ** -0.5, 0.125, ((0, 4), (1, 4)))
    decoder_segments = jax.vmap(lambda own: jnp.searchsorted(jnp.cumsum(ragged(own, DOCS, TOK, TOK // 2, 2)), jnp.arange(TOK), side="right"))(jax.random.split(splits[7], SECTIONS)).reshape((SECTIONS, TOK)).astype(jnp.int32)
    encoder_segments = jax.vmap(lambda own: jnp.searchsorted(jnp.cumsum(ragged(own, DOCS, TE, TE // 2, 2)), jnp.arange(TE), side="right"))(jax.random.split(splits[8], SECTIONS)).reshape((SECTIONS, TE)).astype(jnp.int32)
    return dict(decoder_rows=decoder_rows, encoder_panel=encoder_panel, norm_gain=norm_gain, w_query=w_query, w_key=w_key, w_value=w_value, w_output=w_output, decoder_segments=decoder_segments, encoder_segments=encoder_segments)


def normed_rows(layer_rows, gain):
    widened = layer_rows.astype(jnp.float32)
    mean_square = lax.optimization_barrier(jnp.mean(widened * widened, axis=-1, keepdims=True))
    return (widened * lax.rsqrt(mean_square + 1e-06) * gain.astype(jnp.float32)).astype(jnp.bfloat16)

def attend_head(head_queries, head_keys, head_values, query_ids, key_ids):
    scores = jnp.dot(head_queries, head_keys.T, preferred_element_type=jnp.float32) * HD ** (-0.5)
    matching = query_ids[:, None] == key_ids[None, :]
    row_peak = lax.optimization_barrier(jnp.max(jnp.where(matching, scores, -1e+30), axis=-1, keepdims=True))
    weights = jnp.where(matching, jnp.exp(scores - row_peak), 0.0)
    row_total = lax.optimization_barrier(jnp.sum(weights, axis=-1, keepdims=True))
    summed = jnp.dot(weights.astype(jnp.bfloat16), head_values, preferred_element_type=jnp.float32)
    return (summed / row_total).astype(jnp.bfloat16)

def reference(decoder_rows, encoder_panel, norm_gain, w_query, w_key, w_value, w_output, decoder_segments, encoder_segments):
    results = []
    for section_index in range(SECTIONS):
        layer_rows = decoder_rows[section_index]
        hidden = normed_rows(layer_rows, norm_gain[section_index])
        queries = jnp.dot(hidden, w_query[section_index], preferred_element_type=jnp.float32).astype(jnp.bfloat16)
        key_rows = jnp.dot(encoder_panel[section_index], w_key[section_index], preferred_element_type=jnp.float32).astype(jnp.bfloat16)
        value_rows = jnp.dot(encoder_panel[section_index], w_value[section_index], preferred_element_type=jnp.float32).astype(jnp.bfloat16)
        head_outputs = []
        for head_index in range(HEADS):
            first_col = head_index * HD
            head_outputs.append(attend_head(queries[:, first_col:first_col + HD], key_rows[:, first_col:first_col + HD], value_rows[:, first_col:first_col + HD], decoder_segments[section_index], encoder_segments[section_index]))
        context = jnp.concatenate(head_outputs, axis=1)
        summed = jnp.dot(context, w_output[section_index], preferred_element_type=jnp.float32) + layer_rows.astype(jnp.float32)
        results.append(summed.astype(jnp.bfloat16))
    return jnp.stack(results)
```

```python
import functools
import math

import jax
import jax.numpy as jnp
from jax import lax
from jax.experimental import pallas as pl
from jax.experimental.pallas import tpu as pltpu
from jax.sharding import PartitionSpec as P

HD = 256
AXES = ("section", "seq", "mp")
SHAPE = (4, 2, 4, 2, 2)
CHUNKS = 2
MIB = 1 << 20
F32 = jnp.float32
BF16 = jnp.bfloat16


def route(target):
    pairs = []
    for source in range(math.prod(SHAPE)):
        at, rest = [], source
        for size in reversed(SHAPE):
            at.append(rest % size)
            rest //= size
        there = 0
        for place, size in zip(target(*reversed(at)), SHAPE):
            there = there * size + place % size
        pairs.append((source, there))
    return pairs


CORE = route(lambda x, l, z, h, c: (x, l, z, h, c + 1))
Y_FAR = route(lambda x, l, z, h, c: (x, l, z, h + 1, c))
Y_CUT = route(lambda x, l, z, h, c: (x, l + 1, z, h + 1, c))
Y_LOW = route(lambda x, l, z, h, c: (x, l + 1, z, h, c))
Z_UP = route(lambda x, l, z, h, c: (x, l, z + 1, h, c))
Z_DOWN = route(lambda x, l, z, h, c: (x, l, z - 1, h, c))
X_UP = route(lambda x, l, z, h, c: (x + 1, l, z, h, c))
X_DOWN = route(lambda x, l, z, h, c: (x - 1, l, z, h, c))
X_TWO = route(lambda x, l, z, h, c: (x + 2, l, z, h, c))
X_ORDER = (0, -1, 1, 2)


def send(array, pairs):
    return lax.ppermute(array, AXES, pairs)


def vmem(count):
    return [pl.BlockSpec(memory_space=pltpu.VMEM)] * count


def smem(count):
    return [pl.BlockSpec(memory_space=pltpu.SMEM)] * count


def params(mib):
    return pltpu.CompilerParams(vmem_limit_bytes=mib * MIB)


def normed_rows(layer_rows, gain):
    widened = layer_rows.astype(F32)
    mean_square = jnp.mean(widened * widened, axis=-1, keepdims=True)
    return (widened * lax.rsqrt(mean_square + 1e-06) * gain.astype(F32)).astype(BF16)


def dot(a, b):
    return jnp.dot(a, b, preferred_element_type=F32)


def key_value_kernel(place, b0, b1, b2, b3, w_key, w_value, mine, other, panel):
    section, low, mp = place[0], place[1], place[2]
    for flip, block in enumerate((b0, b1, b2, b3)):
        for step, offset in enumerate(X_ORDER):
            column = ((section + offset + 4) % 4 * 4 + jnp.bitwise_xor(mp, flip)) * 256
            panel[:, pl.ds(pl.multiple_of(column, 256), 256)] = block[step]
    for out, side in ((mine, low), (other, 1 - low)):
        columns = pl.ds(pl.multiple_of(side * HD, HD), HD)
        for at, weight in ((0, w_key), (1, w_value)):
            out[at] = dot(panel[...], weight[:, columns]).astype(BF16)


def key_values(place, blocks, w_key, w_value):
    rows = blocks[0].shape[1]
    out = jax.ShapeDtypeStruct((2, rows, HD), BF16)
    return pl.pallas_call(
        key_value_kernel,
        out_shape=(out, out),
        in_specs=smem(1) + vmem(6),
        out_specs=tuple(vmem(2)),
        scratch_shapes=[pltpu.VMEM((rows, 4096), BF16)],
        compiler_params=params(24),
        cost_estimate=pl.CostEstimate(
            flops=2 * rows * 4096 * 1024, bytes_accessed=8 * MIB + rows * 8192, transcendentals=0
        ),
        name="key_values",
    )(place, *blocks, w_key, w_value)


def query_kernel(place, h0, h1, w_query, mine, other):
    low = place[1]
    rows = h0.shape[0]
    for out, side in ((mine, low), (other, 1 - low)):
        columns = pl.ds(pl.multiple_of(side * HD, HD), HD)
        for at, block in enumerate((h0, h1)):
            out[at * rows : (at + 1) * rows] = dot(block[...], w_query[:, columns]).astype(BF16)


def queries(place, blocks, w_query):
    rows = blocks[0].shape[0] * 2
    out = jax.ShapeDtypeStruct((rows, HD), BF16)
    return pl.pallas_call(
        query_kernel,
        out_shape=(out, out),
        in_specs=smem(1) + vmem(3),
        out_specs=tuple(vmem(2)),
        compiler_params=params(16),
        cost_estimate=pl.CostEstimate(
            flops=2 * rows * 4096 * 512, bytes_accessed=4 * MIB + rows * 8192, transcendentals=0
        ),
        name="queries",
    )(place, *blocks, w_query)


def attend_kernel(pieces, spans, query_span, key_span, query, query_ids, key_ids, *refs):
    parts, (out, peak, total, context) = refs[:pieces], refs[pieces:]
    block = 256

    def one_block(at, _):
        rows = pl.ds(pl.multiple_of(at * block, block), block)
        peak[...] = jnp.full_like(peak, -1e30)
        total[...] = jnp.zeros_like(total)
        context[...] = jnp.zeros_like(context)
        for part, keys_values in enumerate(parts):
            span = spans[part]
            meets = (key_span[0, span] <= query_span[1, at]) & (key_span[1, span] >= query_span[0, at])

            @pl.when(meets)
            def _():
                scores = lax.dot_general(
                    query[rows], keys_values[0], (((1,), (1,)), ((), ())), preferred_element_type=F32
                ) * HD ** (-0.5)
                matching = query_ids[rows] == key_ids[pl.ds(span, 1)]
                scores = jnp.where(matching, scores, -1e30)
                old = peak[...]
                new = jnp.maximum(old, jnp.max(scores, axis=-1, keepdims=True))
                weights = jnp.where(matching, jnp.exp(scores - new), 0.0)
                shrink = jnp.exp(old - new)
                peak[...] = new
                total[...] = total[...] * shrink + jnp.sum(weights, axis=-1, keepdims=True)
                context[...] = context[...] * shrink + dot(weights.astype(BF16), keys_values[1])

        out[rows] = (context[...] / total[...]).astype(BF16)
        return 0

    lax.fori_loop(0, query.shape[0] // block, one_block, 0)


def attend(spans, query_span, key_span, query, query_ids, key_ids, parts):
    rows = query.shape[0]
    return pl.pallas_call(
        functools.partial(attend_kernel, len(parts)),
        out_shape=jax.ShapeDtypeStruct((rows, HD), BF16),
        in_specs=smem(3) + vmem(3 + len(parts)),
        out_specs=vmem(1)[0],
        scratch_shapes=[
            pltpu.VMEM((256, 1), F32),
            pltpu.VMEM((256, 1), F32),
            pltpu.VMEM((256, HD), F32),
        ],
        compiler_params=params(24),
        cost_estimate=pl.CostEstimate(
            flops=2 * rows * 4096 * 256, bytes_accessed=6 * MIB, transcendentals=rows * 1024
        ),
        name="attend",
    )(spans, query_span, key_span, query, query_ids, key_ids, *parts)


def output_kernel(place, mine, other, w_output, out):
    low = place[1]
    first = w_output[pl.ds(pl.multiple_of(low * HD, HD), HD)]
    second = w_output[pl.ds(pl.multiple_of((1 - low) * HD, HD), HD)]
    out[...] = (dot(mine[...], first) + dot(other[...], second)).astype(BF16)


def outputs(place, mine, other, w_output):
    rows = mine.shape[0]
    return pl.pallas_call(
        output_kernel,
        grid=(4,),
        out_shape=jax.ShapeDtypeStruct((rows, 4096), BF16),
        in_specs=smem(1) + vmem(2) + [pl.BlockSpec((512, 1024), lambda i: (0, i))],
        out_specs=pl.BlockSpec((rows, 1024), lambda i: (0, i)),
        compiler_params=params(16),
        cost_estimate=pl.CostEstimate(
            flops=2 * rows * 4096 * 512, bytes_accessed=4 * MIB + rows * 8192, transcendentals=0
        ),
        name="outputs",
    )(place, mine, other, w_output)


def per_device(
    decoder_rows,
    encoder_panel,
    norm_gain,
    w_query,
    w_key,
    w_value,
    w_output,
    decoder_segments,
    encoder_segments,
):
    section = lax.axis_index("section")
    seq = lax.axis_index("seq")
    mp = lax.axis_index("mp")
    low, z = seq // 4, seq % 4
    place = jnp.stack([section, low, mp]).astype(jnp.int32)

    rows = 512 // CHUNKS
    crossed = []
    for chunk in range(CHUNKS):

        def panel_of(offset):
            return lax.dynamic_slice(
                encoder_panel, ((section + offset) % 4, chunk * rows, 0), (1, rows, 256)
            )

        crossed.append(
            jnp.concatenate(
                [
                    panel_of(0),
                    send(panel_of(1), X_UP),
                    send(panel_of(3), X_DOWN),
                    send(panel_of(2), X_TWO),
                ]
            )
        )
    panels = []
    for own in crossed:
        far = send(own, Y_FAR)
        panels.append((own, send(own, CORE), far, send(far, CORE)))

    local_rows = decoder_rows[0]
    hidden = normed_rows(local_rows, norm_gain[0])
    hidden_cut = send(hidden, Y_CUT)
    query_near = queries(place, (hidden, send(hidden, CORE)), w_query[0])
    query_far = queries(place, (hidden_cut, send(hidden_cut, CORE)), w_query[0])
    query_mine = jnp.concatenate([query_near[0], query_far[0]])
    query_other = send(jnp.concatenate([query_near[1], query_far[1]]), Y_LOW)
    query = jnp.concatenate([query_mine, query_other])

    ids_own = decoder_segments[0].reshape(4, 128)
    ids_low = send(ids_own, Y_LOW)
    query_ids = jnp.stack(
        [
            (ids_own if flip_low == 0 else ids_low)[jnp.bitwise_xor(mp, flip)]
            for flip_low, flip in ((0, 0), (0, 1), (1, 2), (1, 3), (1, 0), (1, 1), (0, 2), (0, 3))
        ]
    ).reshape(1024)
    query_blocks = query_ids.reshape(4, 256)
    query_span = jnp.stack([query_blocks.min(axis=1), query_blocks.max(axis=1)])
    key_ids = encoder_segments[0].reshape(8 * CHUNKS, rows)
    key_span = jnp.stack([key_ids[:, 0], key_ids[:, -1]])

    parts, spans = [], []

    def note(part, flip_low, step, chunk):
        parts.append(part)
        spans.append((jnp.bitwise_xor(low, flip_low) * 4 + (z + step) % 4) * CHUNKS + chunk)

    for chunk in range(CHUNKS):
        mine, other = key_values(place, panels[chunk], w_key[0], w_value[0])
        for flip_low, held in ((0, mine), (1, send(other, Y_LOW))):
            below, above = send(held, Z_UP), send(held, Z_DOWN)
            across = jnp.stack([send(below[0], Z_UP), send(above[1], Z_DOWN)])
            note(held, flip_low, 0, chunk)
            note(below, flip_low, 3, chunk)
            note(above, flip_low, 1, chunk)
            note(across, flip_low, 2, chunk)

    context = attend(
        jnp.stack(spans).astype(jnp.int32),
        query_span,
        key_span,
        query,
        query_ids[:, None],
        key_ids,
        parts,
    )

    context_other = send(context[512:], Y_LOW)
    across = outputs(place, context[256:512], context_other[256:], w_output[0])
    near = outputs(place, context[:256], context_other[:256], w_output[0])
    across_sum = (across[:128].astype(F32) + send(across[128:], CORE).astype(F32)).astype(BF16)
    arrived = send(across_sum, Y_CUT)
    near_sum = near[:128].astype(F32) + send(near[128:], CORE).astype(F32)
    summed = near_sum + arrived.astype(F32)
    return (summed + local_rows.astype(F32)).astype(BF16)[None]


def solution(mesh):
    in_specs = (
        P("section", ("seq", "mp"), None),
        P(None, "seq", ("section", "mp")),
        P("section", None),
        P("section", None, "mp"),
        P("section", None, "mp"),
        P("section", None, "mp"),
        P("section", "mp", None),
        P("section", "seq"),
        P("section", None),
    )
    out_specs = P("section", ("seq", "mp"), None)
    return jax.shard_map(
        per_device, mesh=mesh, in_specs=in_specs, out_specs=out_specs, check_vma=False
    )
```

```python
import functools
import math

import jax
import jax.numpy as jnp
from jax import lax
from jax.experimental import pallas as pl
from jax.experimental.pallas import tpu as pltpu
from jax.sharding import PartitionSpec as P

HD = 256
AXES = ("section", "seq", "mp")
SHAPE = (4, 2, 4, 2, 2)
KEYS = 256
ATTEND_ROWS = 512
MIB = 1 << 20
F32 = jnp.float32
BF16 = jnp.bfloat16


def route(target):
    pairs = []
    for source in range(math.prod(SHAPE)):
        at, rest = [], source
        for size in reversed(SHAPE):
            at.append(rest % size)
            rest //= size
        there = 0
        for place, size in zip(target(*reversed(at)), SHAPE):
            there = there * size + place % size
        pairs.append((source, there))
    return pairs


CORE = route(lambda x, l, z, h, c: (x, l, z, h, c + 1))
Y_FAR = route(lambda x, l, z, h, c: (x, l, z, h + 1, c))
Y_CUT = route(lambda x, l, z, h, c: (x, l + 1, z, h + 1, c))
Y_LOW_CORE = route(lambda x, l, z, h, c: (x, l + 1, z, h, c + 1))
Y_LOW = route(lambda x, l, z, h, c: (x, l + 1, z, h, c))
Z_UP = route(lambda x, l, z, h, c: (x, l, z + 1, h, c))
Z_DOWN = route(lambda x, l, z, h, c: (x, l, z - 1, h, c))
X_UP = route(lambda x, l, z, h, c: (x + 1, l, z, h, c))
X_DOWN = route(lambda x, l, z, h, c: (x - 1, l, z, h, c))
X_TWO = route(lambda x, l, z, h, c: (x + 2, l, z, h, c))
X_ORDER = (0, -1, 1, 2)


def send(array, pairs):
    return lax.ppermute(array, AXES, pairs)


def vmem(count):
    return [pl.BlockSpec(memory_space=pltpu.VMEM)] * count


def smem(count):
    return [pl.BlockSpec(memory_space=pltpu.SMEM)] * count


def params(mib):
    return pltpu.CompilerParams(vmem_limit_bytes=mib * MIB)


def normed_rows(layer_rows, gain):
    widened = layer_rows.astype(F32)
    mean_square = jnp.mean(widened * widened, axis=-1, keepdims=True)
    return (widened * lax.rsqrt(mean_square + 1e-06) * gain.astype(F32)).astype(BF16)


def dot(a, b):
    return jnp.dot(a, b, preferred_element_type=F32)


def fetch(source, held, arrived, pieces, piece):
    copies = [
        pltpu.make_async_copy(source.at[piece(at)], held.at[piece(at)], arrived.at[at])
        for at in range(pieces)
    ]
    for copy in copies:
        copy.start()
    return lambda at: copies[at].wait()


def row_piece(at):
    return (pl.ds(at * 1024, 1024),)


def key_value_kernel(place, *refs):
    blocks, (w_key, w_value, mine, other, panel, keys, values, sums, arrived) = refs[:16], refs[16:]
    wait_key = fetch(w_key, keys, arrived.at[0], 4, row_piece)
    wait_value = fetch(w_value, values, arrived.at[1], 4, row_piece)
    for at, block in enumerate(blocks):
        step, flip = divmod(at, 4)
        column = place[3 + step] * 1024 + jnp.bitwise_xor(place[2], flip) * 256
        panel[:, pl.ds(pl.multiple_of(column, 256), 256)] = block[0]
    for step in range(4):
        block = panel[:, step * 1024 : (step + 1) * 1024]
        for at, (wait, held) in enumerate(((wait_key, keys), (wait_value, values))):
            wait(step)
            product = dot(block, held[step * 1024 : (step + 1) * 1024])
            if step == 0:
                sums[at] = product
            else:
                sums[at] += product
    for out, side in ((mine, place[1]), (other, 1 - place[1])):
        for at in range(2):
            out[at] = sums[at, :, pl.ds(pl.multiple_of(side * HD, HD), HD)].astype(BF16)


def hbm(count):
    return [pl.BlockSpec(memory_space=pltpu.HBM)] * count


def key_values(place, blocks, w_key, w_value):
    rows = blocks[0].shape[1]
    out = jax.ShapeDtypeStruct((2, rows, HD), BF16)
    return pl.pallas_call(
        key_value_kernel,
        out_shape=(out, out),
        in_specs=smem(1) + vmem(16) + hbm(2),
        out_specs=tuple(vmem(2)),
        scratch_shapes=[
            pltpu.VMEM((rows, 4096), BF16),
            pltpu.VMEM((4096, 512), BF16),
            pltpu.VMEM((4096, 512), BF16),
            pltpu.VMEM((2, rows, 512), F32),
            pltpu.SemaphoreType.DMA((2, 4)),
        ],
        compiler_params=params(48),
        cost_estimate=pl.CostEstimate(
            flops=2 * rows * 4096 * 1024, bytes_accessed=8 * MIB + rows * 8192, transcendentals=0
        ),
        name="key_values",
    )(place, *blocks, w_key, w_value)


def query_kernel(place, h0, h1, w_query, mine, other, weight, sums, arrived):
    wait = fetch(w_query, weight, arrived, 4, row_piece)
    rows = h0.shape[0]
    for step in range(4):
        span = slice(step * 1024, (step + 1) * 1024)
        wait(step)
        product = dot(jnp.concatenate([h0[:, span], h1[:, span]]), weight[span])
        if step == 0:
            sums[...] = product
        else:
            sums[...] += product
    for out, side in ((mine, place[1]), (other, 1 - place[1])):
        out[...] = sums[:, pl.ds(pl.multiple_of(side * HD, HD), HD)].astype(BF16)


def queries(place, blocks, w_query):
    rows = blocks[0].shape[0]
    out = jax.ShapeDtypeStruct((2 * rows, HD), BF16)
    return pl.pallas_call(
        query_kernel,
        out_shape=(out, out),
        in_specs=smem(1) + vmem(2) + hbm(1),
        out_specs=tuple(vmem(2)),
        scratch_shapes=[
            pltpu.VMEM((4096, 512), BF16),
            pltpu.VMEM((2 * rows, 512), F32),
            pltpu.SemaphoreType.DMA((4,)),
        ],
        compiler_params=params(48),
        cost_estimate=pl.CostEstimate(
            flops=4 * rows * 4096 * 512, bytes_accessed=4 * MIB + rows * 16384, transcendentals=0
        ),
        name="queries",
    )(place, *blocks, w_query)


def attend_kernel(pieces, keys, place, span_ids, *refs):
    ids_own, ids_low, key_ids, near, far_low, near_low, far = refs[:7]
    arrays, outs, (query, ids, scores, peak, total, context) = refs[7:-10], refs[-10:-6], refs[-6:]
    block = ATTEND_ROWS
    scale = HD ** (-0.5) * math.log2(math.e)
    low, mp, z = place[1], place[2], place[7]

    for at, rows in enumerate((near, far_low, near_low, far)):
        query[at * 256 : (at + 1) * 256] = rows[...]
    for at, held in enumerate((ids_own, ids_low)):
        for flip in range(4):
            first = at * block + flip * 128
            row = held[pl.ds(jnp.bitwise_xor(mp, flip), 1)]
            ids[first : first + 128] = jnp.transpose(jnp.broadcast_to(row, (128, 128)))

    def one_block(at, _):
        rows = pl.ds(pl.multiple_of(at * block, block), block)
        lowest, highest_id = span_ids[at, 0], span_ids[at, 1]
        peak[...] = jnp.full_like(peak, -1e30)
        total[...] = jnp.zeros_like(total)
        context[...] = jnp.zeros_like(context)

        def rows_of(held, row):
            array, lead = held
            return arrays[array].at[lead + (pl.ds(row, keys),)]

        def for_each_part(step):
            for part, (flip_low, turn, piece_keys, piece_values, row) in enumerate(pieces):
                first = (jnp.bitwise_xor(low, flip_low) * 4 + (z + turn) % 4) * 512 + row
                meets = (span_ids[2, first] <= highest_id) & (span_ids[2, first + keys - 1] >= lowest)
                pl.when(meets)(
                    functools.partial(
                        step, part, rows_of(piece_keys, row), rows_of(piece_values, row), first
                    )
                )

        def score(part, part_keys, part_values, first):
            product = lax.dot_general(
                query[rows], part_keys[...], (((1,), (1,)), ((), ())), preferred_element_type=F32
            )
            own_ids = ids[rows]
            highest = peak[...]
            for lane in range(0, keys, 128):
                lane_ids = key_ids[:, pl.ds(pl.multiple_of(first + lane, 128), 128)]
                kept = jnp.where(own_ids == lane_ids, product[:, lane : lane + 128] * scale, -1e30)
                scores[part, :, lane : lane + 128] = kept
                highest = jnp.maximum(highest, kept)
            peak[...] = highest

        for_each_part(score)
        highest = jnp.max(peak[...], axis=-1, keepdims=True)

        def weigh(part, part_keys, part_values, first):
            weights = jnp.exp2(scores[part] - highest)
            sums = total[...]
            for lane in range(0, keys, 128):
                sums = sums + weights[:, lane : lane + 128]
            total[...] = sums
            context[...] += dot(weights.astype(BF16), part_values[...])

        for_each_part(weigh)
        whole = jnp.sum(total[...], axis=-1, keepdims=True)
        context[...] = context[...] / whole

        mine, core, beside, beside_core = outs

        @pl.when(at == 0)
        def _():
            mine[0:128] = context[0:128].astype(BF16)
            core[0:128] = context[128:256].astype(BF16)
            beside[128:256] = context[256:384].astype(BF16)
            beside_core[128:256] = context[384:512].astype(BF16)

        @pl.when(at == 1)
        def _():
            beside[0:128] = context[0:128].astype(BF16)
            beside_core[0:128] = context[128:256].astype(BF16)
            mine[128:256] = context[256:384].astype(BF16)
            core[128:256] = context[384:512].astype(BF16)

        return 0

    lax.fori_loop(0, 2, one_block, 0)


def attend(keys, pieces, arrays, place, span_ids, ids_own, ids_low, key_ids, blocks):
    out = jax.ShapeDtypeStruct((256, HD), BF16)
    return pl.pallas_call(
        functools.partial(attend_kernel, pieces, keys),
        out_shape=(out,) * 4,
        in_specs=smem(2) + vmem(7 + len(arrays)),
        out_specs=tuple(vmem(4)),
        scratch_shapes=[
            pltpu.VMEM((2 * ATTEND_ROWS, HD), BF16),
            pltpu.VMEM((2 * ATTEND_ROWS, 128), jnp.int32),
            pltpu.VMEM((len(pieces), ATTEND_ROWS, keys), F32),
            pltpu.VMEM((ATTEND_ROWS, 128), F32),
            pltpu.VMEM((ATTEND_ROWS, 128), F32),
            pltpu.VMEM((ATTEND_ROWS, HD), F32),
        ],
        compiler_params=params(28),
        cost_estimate=pl.CostEstimate(
            flops=4 * 1024 * 4096 * 256, bytes_accessed=6 * MIB, transcendentals=1024 * 1024
        ),
        name="attend",
    )(place, span_ids, ids_own, ids_low, key_ids, *blocks, *arrays)


def output_kernel(row, first, place, c0, c1, c2, c3, w_own, w_core, *refs):
    residual, (out, weight, arrived) = refs[:-3], refs[-3:]
    pieces = out.shape[1] // 512
    copies = [
        [
            pltpu.make_async_copy(
                source.at[:, pl.ds(first + at * 512, 512)], weight.at[core, at], arrived.at[core, at]
            )
            for core, source in enumerate((w_own, w_core))
        ]
        for at in range(pieces)
    ]
    for pair in copies:
        for copy in pair:
            copy.start()
    span = slice(row, row + 128)
    low = place[1]
    left = jnp.concatenate([c0[span], c2[span]], axis=1)
    left_core = jnp.concatenate([c1[span], c3[span]], axis=1)
    swapped = jnp.concatenate([c2[span], c0[span]], axis=1)
    swapped_core = jnp.concatenate([c3[span], c1[span]], axis=1)
    left = jnp.where(low == 0, left, swapped)
    left_core = jnp.where(low == 0, left_core, swapped_core)
    for at, pair in enumerate(copies):
        columns = slice(at * 512, (at + 1) * 512)
        for copy in pair:
            copy.wait()
        summed = dot(left, weight[0, at]) + dot(left_core, weight[1, at])
        for rows in residual:
            summed = summed + rows[:, columns].astype(F32)
        out[:, columns] = summed.astype(out.dtype)


def outputs(place, contexts, w_own, w_core, row, part, parts, residual=()):
    width = 4096 // parts
    return pl.pallas_call(
        functools.partial(output_kernel, row, part * width),
        out_shape=jax.ShapeDtypeStruct((128, width), F32 if residual else BF16),
        in_specs=smem(1) + vmem(4) + hbm(2) + vmem(len(residual)),
        out_specs=vmem(1)[0],
        scratch_shapes=[
            pltpu.VMEM((2, width // 512, 512, 512), BF16),
            pltpu.SemaphoreType.DMA((2, width // 512)),
        ],
        compiler_params=params(48),
        cost_estimate=pl.CostEstimate(
            flops=2 * 256 * width * 1024, bytes_accessed=width * 2048, transcendentals=0
        ),
        name="outputs",
    )(place, *contexts, w_own, w_core, *residual)


def per_device(
    decoder_rows,
    encoder_panel,
    norm_gain,
    w_query,
    w_key,
    w_value,
    w_output,
    decoder_segments,
    encoder_segments,
):
    section = lax.axis_index("section")
    seq = lax.axis_index("seq")
    mp = lax.axis_index("mp")
    low, z = seq // 4, seq % 4
    place = jnp.stack([section, low, mp] + [(section + offset) % 4 for offset in X_ORDER] + [z]).astype(
        jnp.int32
    )

    def panel_of(offset, first, count):
        return lax.dynamic_slice(
            encoder_panel, ((section + offset) % 4, first, 0), (1, count, 256)
        )

    own = panel_of(0, 0, 512)
    own_far = send(own, Y_FAR)
    crossed = [
        send(panel_of(offset, 0, 512), pairs) for offset, pairs in ((1, X_UP), (3, X_DOWN), (2, X_TWO))
    ]
    crossed[0], own_far = lax.optimization_barrier((crossed[0], own_far))
    panels = [own] + crossed
    fars = [own_far] + [send(block, Y_FAR) for block in crossed]

    local_rows = decoder_rows[0]
    hidden = normed_rows(local_rows, norm_gain[0])
    near_mine, near_other = queries(place, (hidden, send(hidden, CORE)), w_query[0])

    ids_own = decoder_segments[0].reshape(4, 128)
    ids_low = send(ids_own, Y_LOW)
    ends = jnp.stack([jnp.stack([ids[0, 0], ids[3, 127]]) for ids in (ids_own, ids_low)])
    span_ids = jnp.concatenate([jnp.pad(ends, ((0, 0), (0, 4094))), encoder_segments])
    w_core = send(w_output[0], CORE)

    near_mine, near_other, ids_low, span_ids, fars[1] = lax.optimization_barrier(
        (near_mine, near_other, ids_low, span_ids, fars[1])
    )
    blocks = []
    for near, far in zip(panels, fars):
        blocks += [near, send(near, CORE), far, send(far, CORE)]
    mine, other = key_values(place, blocks, w_key[0], w_value[0])

    below_0, above_0 = send(mine, Z_UP), send(mine, Z_DOWN)
    theirs, below_0, above_0 = lax.optimization_barrier((send(other, Y_LOW), below_0, above_0))
    below_1, above_1 = send(theirs, Z_UP), send(theirs, Z_DOWN)
    across_0 = (send(below_0[0], Z_UP), send(above_0[1], Z_DOWN))
    hidden, _ = lax.optimization_barrier((hidden, fars[3]))
    hidden_cut = send(hidden, Y_CUT)
    hidden_cut, below_1, above_1 = lax.optimization_barrier((hidden_cut, below_1, above_1))

    across_1 = (send(below_1[0], Z_UP), send(above_1[1], Z_DOWN))

    far_mine, far_other = queries(place, (hidden_cut, send(hidden_cut, CORE)), w_query[0])
    blocks = (near_mine, send(far_other, Y_LOW), send(near_other, Y_LOW), far_mine)

    arrays, pieces = [], []
    for flip_low, (held, below, above, across) in enumerate(
        ((mine, below_0, above_0, across_0), (theirs, below_1, above_1, across_1))
    ):
        base = len(arrays)
        arrays.extend([held, below, above, *across])
        for turn, keys, values in (
            (0, (base, (0,)), (base, (1,))),
            (3, (base + 1, (0,)), (base + 1, (1,))),
            (1, (base + 2, (0,)), (base + 2, (1,))),
            (2, (base + 3, ()), (base + 4, ())),
        ):
            for row in range(0, 512, KEYS):
                pieces.append((flip_low, turn, keys, values, row))

    contexts = attend(
        KEYS, pieces, arrays, place, span_ids, ids_own, ids_low, encoder_segments, blocks
    )

    contexts = (contexts[0],) + tuple(
        send(context, pairs) for context, pairs in zip(contexts[1:], (CORE, Y_LOW, Y_LOW_CORE))
    )
    w_own = w_output[0]
    arrived = [
        send(outputs(place, contexts, w_own, w_core, 128, part, 2), Y_CUT) for part in range(2)
    ]
    near = outputs(place, contexts, w_own, w_core, 0, 0, 1, (local_rows,))
    return (near + jnp.concatenate(arrived, axis=1).astype(F32)).astype(BF16)[None]


def solution(mesh):
    in_specs = (
        P("section", ("seq", "mp"), None),
        P(None, "seq", ("section", "mp")),
        P("section", None),
        P("section", None, "mp"),
        P("section", None, "mp"),
        P("section", None, "mp"),
        P("section", "mp", None),
        P("section", "seq"),
        P("section", None),
    )
    out_specs = P("section", ("seq", "mp"), None)
    return jax.shard_map(
        per_device, mesh=mesh, in_specs=in_specs, out_specs=out_specs, check_vma=False
    )
```

```python
import functools
import math

import jax
import jax.numpy as jnp
from jax import lax
from jax.experimental import pallas as pl
from jax.experimental.pallas import tpu as pltpu
from jax.sharding import PartitionSpec as P

HD = 256
AXES = ("section", "seq", "mp")
SHAPE = (4, 2, 4, 2, 2)
KEYS = 256
ATTEND_ROWS = 512
MIB = 1 << 20
F32 = jnp.float32
BF16 = jnp.bfloat16


def route(target):
    pairs = []
    for source in range(math.prod(SHAPE)):
        at, rest = [], source
        for size in reversed(SHAPE):
            at.append(rest % size)
            rest //= size
        there = 0
        for place, size in zip(target(*reversed(at)), SHAPE):
            there = there * size + place % size
        pairs.append((source, there))
    return pairs


CORE = route(lambda x, l, z, h, c: (x, l, z, h, c + 1))
Y_FAR = route(lambda x, l, z, h, c: (x, l, z, h + 1, c))
Y_CUT = route(lambda x, l, z, h, c: (x, l + 1, z, h + 1, c))
Y_LOW_CORE = route(lambda x, l, z, h, c: (x, l + 1, z, h, c + 1))
Y_LOW = route(lambda x, l, z, h, c: (x, l + 1, z, h, c))
Z_UP = route(lambda x, l, z, h, c: (x, l, z + 1, h, c))
Z_DOWN = route(lambda x, l, z, h, c: (x, l, z - 1, h, c))
X_UP = route(lambda x, l, z, h, c: (x + 1, l, z, h, c))
X_DOWN = route(lambda x, l, z, h, c: (x - 1, l, z, h, c))
X_TWO = route(lambda x, l, z, h, c: (x + 2, l, z, h, c))
X_ORDER = (0, -1, 1, 2)
W_PIECES = (
    (0, 0, 0, 64, 0),
    (0, 0, 3, 64, 1),
    (0, 0, 1, 64, 2),
    (0, 0, 2, 32, 3),
    (0, 32, 2, 32, 4),
    (1, 0, 0, 64, 5),
    (1, 0, 3, 64, 6),
    (1, 0, 1, 64, 7),
    (1, 0, 2, 64, 8),
)
X_GROUPS = ((0,), (1, 2), (3,))


def send(array, pairs):
    return lax.ppermute(array, AXES, pairs)


def vmem(count):
    return [pl.BlockSpec(memory_space=pltpu.VMEM)] * count


def smem(count):
    return [pl.BlockSpec(memory_space=pltpu.SMEM)] * count


def params(mib):
    return pltpu.CompilerParams(vmem_limit_bytes=mib * MIB)


def normed_rows(layer_rows, gain):
    widened = layer_rows.astype(F32)
    mean_square = jnp.mean(widened * widened, axis=-1, keepdims=True)
    return (widened * lax.rsqrt(mean_square + 1e-06) * gain.astype(F32)).astype(BF16)


def dot(a, b):
    return jnp.dot(a, b, preferred_element_type=F32)


def fetch(source, held, arrived, pieces, piece):
    copies = [
        pltpu.make_async_copy(source.at[piece(at)], held.at[piece(at)], arrived.at[at])
        for at in range(pieces)
    ]
    for copy in copies:
        copy.start()
    return lambda at: copies[at].wait()


def row_piece(at):
    return (pl.ds(at * 1024, 1024),)


def key_value_kernel(place, *refs):
    blocks, (w_key, w_value, mine, other, panel, keys, values, sums, arrived) = refs[:12], refs[12:]
    wait_key = fetch(w_key, keys, arrived.at[0], 4, row_piece)
    wait_value = fetch(w_value, values, arrived.at[1], 4, row_piece)
    for at, block in enumerate(blocks):
        group, flip = divmod(at, 4)
        for lead, step in enumerate(X_GROUPS[group]):
            column = place[3 + step] * 1024 + jnp.bitwise_xor(place[2], flip) * 256
            panel[:, pl.ds(pl.multiple_of(column, 256), 256)] = block[lead]
    for step in range(4):
        block = panel[:, step * 1024 : (step + 1) * 1024]
        for at, (wait, held) in enumerate(((wait_key, keys), (wait_value, values))):
            wait(step)
            product = dot(block, held[step * 1024 : (step + 1) * 1024])
            if step == 0:
                sums[at] = product
            else:
                sums[at] += product
    for out, side in ((mine, place[1]), (other, 1 - place[1])):
        for at in range(2):
            out[at] = sums[at, :, pl.ds(pl.multiple_of(side * HD, HD), HD)].astype(BF16)


def hbm(count):
    return [pl.BlockSpec(memory_space=pltpu.HBM)] * count


def key_values(place, blocks, w_key, w_value):
    rows = blocks[0].shape[1]
    out = jax.ShapeDtypeStruct((2, rows, HD), BF16)
    return pl.pallas_call(
        key_value_kernel,
        out_shape=(out, out),
        in_specs=smem(1) + vmem(12) + hbm(2),
        out_specs=tuple(vmem(2)),
        scratch_shapes=[
            pltpu.VMEM((rows, 4096), BF16),
            pltpu.VMEM((4096, 512), BF16),
            pltpu.VMEM((4096, 512), BF16),
            pltpu.VMEM((2, rows, 512), F32),
            pltpu.SemaphoreType.DMA((2, 4)),
        ],
        compiler_params=params(48),
        cost_estimate=pl.CostEstimate(
            flops=2 * rows * 4096 * 1024, bytes_accessed=8 * MIB + rows * 8192, transcendentals=0
        ),
        name="key_values",
    )(place, *blocks, w_key, w_value)


def query_kernel(place, h0, h1, w_query, mine, other, weight, sums, arrived):
    wait = fetch(w_query, weight, arrived, 4, row_piece)
    rows = h0.shape[0]
    for step in range(4):
        span = slice(step * 1024, (step + 1) * 1024)
        wait(step)
        product = dot(jnp.concatenate([h0[:, span], h1[:, span]]), weight[span])
        if step == 0:
            sums[...] = product
        else:
            sums[...] += product
    for out, side in ((mine, place[1]), (other, 1 - place[1])):
        out[...] = sums[:, pl.ds(pl.multiple_of(side * HD, HD), HD)].astype(BF16)


def queries(place, blocks, w_query):
    rows = blocks[0].shape[0]
    out = jax.ShapeDtypeStruct((2 * rows, HD), BF16)
    return pl.pallas_call(
        query_kernel,
        out_shape=(out, out),
        in_specs=smem(1) + vmem(2) + hbm(1),
        out_specs=tuple(vmem(2)),
        scratch_shapes=[
            pltpu.VMEM((4096, 512), BF16),
            pltpu.VMEM((2 * rows, 512), F32),
            pltpu.SemaphoreType.DMA((4,)),
        ],
        compiler_params=params(48),
        cost_estimate=pl.CostEstimate(
            flops=4 * rows * 4096 * 512, bytes_accessed=8 * MIB, transcendentals=0
        ),
        name="queries",
    )(place, *blocks, w_query)


def attend_kernel(pieces, keys, place, own_span, low_span, key_span, *refs):
    ids_own, ids_low, key_ids, near, far_low, near_low, far = refs[:7]
    arrays, outs, (query, ids, scores, peak, total, context) = refs[7:-10], refs[-10:-6], refs[-6:]
    block = ATTEND_ROWS
    scale = HD ** (-0.5) * math.log2(math.e)
    low, mp, z = place[1], place[2], place[7]

    for at, rows in enumerate((near, far_low, near_low, far)):
        query[at * 256 : (at + 1) * 256] = rows[...]
    for at, held in enumerate((ids_own, ids_low)):
        for flip in range(4):
            first = at * block + flip * 128
            row = held[pl.ds(jnp.bitwise_xor(mp, flip), 1)]
            ids[first : first + 128] = jnp.transpose(jnp.broadcast_to(row, (128, 128)))

    def one_block(at, _):
        rows = pl.ds(pl.multiple_of(at * block, block), block)
        lowest = jnp.where(at == 0, own_span[0, 0], low_span[0, 0])
        highest_id = jnp.where(at == 0, own_span[3, 127], low_span[3, 127])
        peak[...] = jnp.full_like(peak, -1e30)
        total[...] = jnp.zeros_like(total)
        context[...] = jnp.zeros_like(context)

        def rows_of(held):
            array, lead, row = held
            return arrays[array].at[lead + (pl.ds(row, keys),)]

        def for_each_part(step):
            for part, (flip_low, turn, row, piece_keys, piece_values) in enumerate(pieces):
                first = (jnp.bitwise_xor(low, flip_low) * 4 + (z + turn) % 4) * 512 + row
                meets = (key_span[0, first] <= highest_id) & (key_span[0, first + keys - 1] >= lowest)
                pl.when(meets)(
                    functools.partial(step, part, rows_of(piece_keys), rows_of(piece_values), first)
                )

        def score(part, part_keys, part_values, first):
            product = lax.dot_general(
                query[rows], part_keys[...], (((1,), (1,)), ((), ())), preferred_element_type=F32
            )
            own_ids = ids[rows]
            highest = peak[...]
            for lane in range(0, keys, 128):
                lane_ids = key_ids[:, pl.ds(pl.multiple_of(first + lane, 128), 128)]
                kept = jnp.where(own_ids == lane_ids, product[:, lane : lane + 128] * scale, -1e30)
                scores[part, :, lane : lane + 128] = kept
                highest = jnp.maximum(highest, kept)
            peak[...] = highest

        for_each_part(score)
        highest = jnp.max(peak[...], axis=-1, keepdims=True)

        def weigh(part, part_keys, part_values, first):
            weights = jnp.exp2(scores[part] - highest)
            sums = total[...]
            for lane in range(0, keys, 128):
                sums = sums + weights[:, lane : lane + 128]
            total[...] = sums
            context[...] += dot(weights.astype(BF16), part_values[...])

        for_each_part(weigh)
        whole = jnp.sum(total[...], axis=-1, keepdims=True)
        context[...] = context[...] / whole

        for tile in range(2):

            @pl.when(at == tile)
            def _():
                outs[2 * tile][...] = context[0:256].astype(BF16)
                outs[2 * tile + 1][...] = context[256:512].astype(BF16)

        return 0

    lax.fori_loop(0, 2, one_block, 0)


def attend(keys, pieces, arrays, place, ids_own, ids_low, key_ids, blocks):
    out = jax.ShapeDtypeStruct((256, HD), BF16)
    return pl.pallas_call(
        functools.partial(attend_kernel, pieces, keys),
        out_shape=(out,) * 4,
        in_specs=smem(4) + vmem(7 + len(arrays)),
        out_specs=tuple(vmem(4)),
        scratch_shapes=[
            pltpu.VMEM((2 * ATTEND_ROWS, HD), BF16),
            pltpu.VMEM((2 * ATTEND_ROWS, 128), jnp.int32),
            pltpu.VMEM((len(pieces), ATTEND_ROWS, keys), F32),
            pltpu.VMEM((ATTEND_ROWS, 128), F32),
            pltpu.VMEM((ATTEND_ROWS, 128), F32),
            pltpu.VMEM((ATTEND_ROWS, HD), F32),
        ],
        compiler_params=params(28),
        cost_estimate=pl.CostEstimate(
            flops=4 * 1024 * 4096 * 256, bytes_accessed=6 * MIB, transcendentals=1024 * 1024
        ),
        name="attend",
    )(place, ids_own, ids_low, key_ids, ids_own, ids_low, key_ids, *blocks, *arrays)


def output_kernel(first, place, c0, c1, c2, c3, w_own, *refs):
    pieces, (out, weight, arrived) = refs[:-3], refs[-3:]
    low, z, width = place[1], place[7], weight.shape[3]
    steps = out.shape[1] // width
    copies = []
    for step in range(steps):
        columns = pl.ds(first + step * width, width)
        moves = [(w_own.at[:, columns], weight.at[step, 0])]
        for head, row, turn, count, at in W_PIECES:
            start = jnp.bitwise_xor(low, head) * HD + (z + turn) % 4 * 64 + row
            target = weight.at[step, 1, pl.ds(pl.multiple_of(start, 32), count)]
            moves.append((pieces[at].at[:, columns], target))
        copies.append(
            [
                pltpu.make_async_copy(source, target, arrived.at[step, at])
                for at, (source, target) in enumerate(moves)
            ]
        )
    for moves in copies:
        for copy in moves:
            copy.start()
    near = jnp.where(low == 0, jnp.concatenate([c0[...], c2[...]], 1), jnp.concatenate([c2[...], c0[...]], 1))
    far = jnp.where(low == 0, jnp.concatenate([c1[...], c3[...]], 1), jnp.concatenate([c3[...], c1[...]], 1))
    for step, moves in enumerate(copies):
        for copy in moves:
            copy.wait()
        summed = dot(near, weight[step, 0]) + dot(far, weight[step, 1])
        out[:, step * width : (step + 1) * width] = summed.astype(out.dtype)


def outputs(place, contexts, w_own, pieces, part, parts):
    width, step = 4096 // parts, 512
    return pl.pallas_call(
        functools.partial(output_kernel, part * width),
        out_shape=jax.ShapeDtypeStruct((256, width), BF16),
        in_specs=smem(1) + vmem(4) + hbm(1 + len(pieces)),
        out_specs=vmem(1)[0],
        scratch_shapes=[
            pltpu.VMEM((width // step, 2, 512, step), BF16),
            pltpu.SemaphoreType.DMA((width // step, 1 + len(pieces))),
        ],
        compiler_params=params(48),
        cost_estimate=pl.CostEstimate(
            flops=2 * 256 * width * 1024, bytes_accessed=width * 2048, transcendentals=0
        ),
        name="outputs",
    )(place, *contexts, w_own, *pieces)


def per_device(
    decoder_rows,
    encoder_panel,
    norm_gain,
    w_query,
    w_key,
    w_value,
    w_output,
    decoder_segments,
    encoder_segments,
):
    section = lax.axis_index("section")
    seq = lax.axis_index("seq")
    mp = lax.axis_index("mp")
    low, z = seq // 4, seq % 4
    place = jnp.stack([section, low, mp] + [(section + offset) % 4 for offset in X_ORDER] + [z]).astype(
        jnp.int32
    )

    ids_own = decoder_segments[0].reshape(4, 128)

    def panel_of(offset, first, count):
        return lax.dynamic_slice(
            encoder_panel, ((section + offset) % 4, first, 0), (1, count, 256)
        )

    w_own = w_output[0]

    def rows_for_cut(head, turn):
        return lax.dynamic_slice(w_own, (head * HD + (z + turn) % 4 * 64, 0), (64, 4096))

    piece = send(rows_for_cut(1 - low, 0), Y_CUT)
    own = panel_of(0, 0, 512)
    up, down = send(panel_of(1, 0, 512), X_UP), send(panel_of(3, 0, 512), X_DOWN)
    local_rows = decoder_rows[0]
    hidden = normed_rows(local_rows, norm_gain[0])
    up, down, own_far, two, hidden, piece, w_own = lax.optimization_barrier(
        (up, down, send(own, Y_FAR), panel_of(2, 0, 512), hidden, piece, w_own)
    )
    pair = jnp.concatenate([up, down])
    two, pair_far, piece_below, piece_above, cut_1, cut_2 = lax.optimization_barrier(
        (
            send(two, X_TWO),
            send(pair, Y_FAR),
            send(piece, Z_UP),
            send(piece, Z_DOWN),
            rows_for_cut(low, 1),
            rows_for_cut(low, 2),
        )
    )
    near_mine, near_other = queries(place, (hidden, send(hidden, CORE)), w_query[0])
    far_rows = [piece, piece_below, piece_above]
    far_rows += [send(piece_below[:32], Z_UP), send(piece_above[32:], Z_DOWN)]
    two_far, ids_low, near_mine, near_other, *far_rows = lax.optimization_barrier(
        (send(two, Y_FAR), send(ids_own, Y_LOW), near_mine, near_other, *far_rows)
    )
    panels, fars = [own, pair, two], [own_far, pair_far, two_far]


    blocks = []
    for near, far in zip(panels, fars):
        blocks += [near, send(near, CORE), far, send(far, CORE)]
    mine, other = key_values(place, blocks, w_key[0], w_value[0])

    hidden, _ = lax.optimization_barrier((hidden, two_far))
    hidden_cut = send(hidden, Y_CUT)
    below_0, above_0 = send(mine, Z_UP), send(mine, Z_DOWN)
    theirs, below_0, above_0, hidden_cut, piece, cut_1 = lax.optimization_barrier(
        (send(other, Y_LOW), below_0, above_0, hidden_cut, far_rows[0], cut_1)
    )
    below_1, above_1 = send(theirs, Z_UP), send(theirs, Z_DOWN)

    far_mine, far_other = queries(place, (hidden_cut, send(hidden_cut, CORE)), w_query[0])
    other_0, other_1 = send(piece, Y_LOW), send(cut_1, Y_CUT)
    below_1, above_1, far_mine, far_other, other_0, other_1, piece, cut_2 = (
        lax.optimization_barrier(
            (below_1, above_1, far_mine, far_other, other_0, other_1, far_rows[1], cut_2)
        )
    )
    across_keys = send(jnp.concatenate([below_0[0], below_1[0]]), Z_UP)
    across_values = send(jnp.concatenate([above_0[1], above_1[1]]), Z_DOWN)
    far_rows += [other_0, send(piece, Y_LOW), other_1, send(cut_2, Y_CUT)]

    blocks = (near_mine, send(far_other, Y_LOW), send(near_other, Y_LOW), far_mine)

    arrays, pieces = [across_keys, across_values], []
    for flip_low, (held, below, above) in enumerate(
        ((mine, below_0, above_0), (theirs, below_1, above_1))
    ):
        for turn, whole in ((0, held), (3, below), (1, above)):
            at = len(arrays)
            arrays.append(whole)
            for row in range(0, 512, KEYS):
                pieces.append((flip_low, turn, row, (at, (0,), row), (at, (1,), row)))
        for row in range(0, 512, KEYS):
            held_row = flip_low * 512 + row
            pieces.append((flip_low, 2, row, (0, (), held_row), (1, (), held_row)))

    contexts = attend(
        KEYS, pieces, arrays, place, ids_own, ids_low, encoder_segments, blocks
    )

    contexts = (contexts[0],) + tuple(
        send(context, pairs) for context, pairs in zip(contexts[1:], (Y_FAR, Y_LOW, Y_CUT))
    )
    summed = []
    for part in range(2):
        both = outputs(place, contexts, w_own, far_rows, part, 2)
        summed.append(both[:128].astype(F32) + send(both[128:], CORE).astype(F32))
    return (jnp.concatenate(summed, axis=1) + local_rows.astype(F32)).astype(BF16)[None]


def solution(mesh):
    in_specs = (
        P("section", ("seq", "mp"), None),
        P(None, "seq", ("section", "mp")),
        P("section", None),
        P("section", None, "mp"),
        P("section", None, "mp"),
        P("section", None, "mp"),
        P("section", "mp", None),
        P("section", "seq"),
        P("section", None),
    )
    out_specs = P("section", ("seq", "mp"), None)
    return jax.shard_map(
        per_device, mesh=mesh, in_specs=in_specs, out_specs=out_specs, check_vma=False
    )
```

```python
import functools
import math

import jax
import jax.numpy as jnp
from jax import lax
from jax.experimental import pallas as pl
from jax.experimental.pallas import tpu as pltpu
from jax.sharding import PartitionSpec as P

HD = 256
AXES = ("section", "seq", "mp")
SHAPE = (4, 2, 4, 2, 2)
KEYS = 256
ATTEND_ROWS = 512
MIB = 1 << 20
F32 = jnp.float32
BF16 = jnp.bfloat16


def route(target):
    pairs = []
    for source in range(math.prod(SHAPE)):
        at, rest = [], source
        for size in reversed(SHAPE):
            at.append(rest % size)
            rest //= size
        there = 0
        for place, size in zip(target(*reversed(at)), SHAPE):
            there = there * size + place % size
        pairs.append((source, there))
    return pairs


CORE = route(lambda x, l, z, h, c: (x, l, z, h, c + 1))
Y_FAR = route(lambda x, l, z, h, c: (x, l, z, h + 1, c))
Y_CUT = route(lambda x, l, z, h, c: (x, l + 1, z, h + 1, c))
Y_LOW_CORE = route(lambda x, l, z, h, c: (x, l + 1, z, h, c + 1))
Y_LOW = route(lambda x, l, z, h, c: (x, l + 1, z, h, c))
Z_UP = route(lambda x, l, z, h, c: (x, l, z + 1, h, c))
Z_DOWN = route(lambda x, l, z, h, c: (x, l, z - 1, h, c))
X_UP = route(lambda x, l, z, h, c: (x + 1, l, z, h, c))
X_DOWN = route(lambda x, l, z, h, c: (x - 1, l, z, h, c))
X_TWO = route(lambda x, l, z, h, c: (x + 2, l, z, h, c))
X_ORDER = (0, -1, 1, 2)
W_PIECES = (
    (0, 0, 0, 64, 0),
    (0, 0, 3, 64, 1),
    (0, 0, 1, 64, 2),
    (0, 0, 2, 32, 3),
    (0, 32, 2, 32, 4),
    (1, 0, 0, 64, 5),
    (1, 0, 3, 64, 6),
    (1, 0, 1, 64, 7),
    (1, 0, 2, 64, 8),
)
X_GROUPS = ((0,), (1, 2), (3,))


def send(array, pairs):
    return lax.ppermute(array, AXES, pairs)


def vmem(count):
    return [pl.BlockSpec(memory_space=pltpu.VMEM)] * count


def smem(count):
    return [pl.BlockSpec(memory_space=pltpu.SMEM)] * count


def params(mib):
    return pltpu.CompilerParams(vmem_limit_bytes=mib * MIB)


def normed_rows(layer_rows, gain):
    widened = layer_rows.astype(F32)
    mean_square = jnp.mean(widened * widened, axis=-1, keepdims=True)
    return (widened * lax.rsqrt(mean_square + 1e-06) * gain.astype(F32)).astype(BF16)


def dot(a, b):
    return jnp.dot(a, b, preferred_element_type=F32)


def fetch(source, held, arrived, pieces, piece):
    copies = [
        pltpu.make_async_copy(source.at[piece(at)], held.at[piece(at)], arrived.at[at])
        for at in range(pieces)
    ]
    for copy in copies:
        copy.start()
    return lambda at: copies[at].wait()


def row_piece(at):
    return (pl.ds(at * 1024, 1024),)


def key_value_kernel(steps, place, *refs):
    count = 4 * len(set(group for group, _, _ in steps))
    blocks, refs = refs[:count], refs[count:]
    w_key, w_value, refs = refs[0], refs[1], refs[2:]
    sums, refs = (None, refs) if steps[0][2] == 0 else (refs[0], refs[1:])
    keys, values, arrived = refs[-3:]
    copies = []
    for at, (_, _, step) in enumerate(steps):
        for flip in range(4):
            row = place[3 + step] * 1024 + jnp.bitwise_xor(place[2], flip) * 256
            source = pl.ds(pl.multiple_of(row, 256), 256)
            target = pl.ds(at * 1024 + flip * 256, 256)
            for which, (weight, held) in enumerate(((w_key, keys), (w_value, values))):
                copies.append(
                    pltpu.make_async_copy(
                        weight.at[source], held.at[target], arrived.at[which, at * 4 + flip]
                    )
                )
    for copy in copies:
        copy.start()
    if sums is None:
        total = refs[0]
    else:
        mine, other, total = refs[:3]
        total[...] = sums[...]
    first = min(group for group, _, _ in steps)
    for at, (group, lead, step) in enumerate(steps):
        panel = jnp.concatenate(
            [blocks[(group - first) * 4 + flip][lead] for flip in range(4)], axis=1
        )
        for copy in copies[at * 8 : at * 8 + 8]:
            copy.wait()
        for which, held in enumerate((keys, values)):
            for side in range(2):
                columns = slice(side * HD, (side + 1) * HD)
                product = dot(panel, held[at * 1024 : (at + 1) * 1024, columns])
                if step == 0:
                    total[which, :, columns] = product
                else:
                    total[which, :, columns] += product
    if sums is not None:
        for side in range(2):

            @pl.when(place[1] == side)
            def _():
                mine[...] = total[:, :, side * HD : (side + 1) * HD].astype(BF16)
                other[...] = total[:, :, (1 - side) * HD : (2 - side) * HD].astype(BF16)


def hbm(count):
    return [pl.BlockSpec(memory_space=pltpu.HBM)] * count


def key_values(place, blocks, w_key, w_value, steps, sums=()):
    rows = blocks[0].shape[1]
    total = (2, rows, 512)
    out = jax.ShapeDtypeStruct((2, rows, HD), BF16)
    depth = 1024 * len(steps)
    return pl.pallas_call(
        functools.partial(key_value_kernel, steps),
        out_shape=(out, out) if sums else jax.ShapeDtypeStruct(total, F32),
        in_specs=smem(1) + vmem(len(blocks)) + hbm(2) + vmem(len(sums)),
        out_specs=tuple(vmem(2)) if sums else vmem(1)[0],
        scratch_shapes=([pltpu.VMEM(total, F32)] if sums else [])
        + [
            pltpu.VMEM((depth, 512), BF16),
            pltpu.VMEM((depth, 512), BF16),
            pltpu.SemaphoreType.DMA((2, 4 * len(steps))),
        ],
        compiler_params=params(48),
        cost_estimate=pl.CostEstimate(
            flops=2 * rows * depth * 1024, bytes_accessed=depth * 3072, transcendentals=0
        ),
        name="key_values",
    )(place, *blocks, w_key, w_value, *sums)


def query_kernel(place, h0, h1, w_query, mine, other, weight, sums, arrived):
    wait = fetch(w_query, weight, arrived, 4, row_piece)
    for step in range(4):
        span = slice(step * 1024, (step + 1) * 1024)
        rows = jnp.concatenate([h0[:, span], h1[:, span]])
        wait(step)
        for side in range(2):
            columns = slice(side * HD, (side + 1) * HD)
            product = dot(rows, weight[span, columns])
            if step == 0:
                sums[:, columns] = product
            else:
                sums[:, columns] += product
    for side in range(2):

        @pl.when(place[1] == side)
        def _():
            mine[...] = sums[:, side * HD : (side + 1) * HD].astype(BF16)
            other[...] = sums[:, (1 - side) * HD : (2 - side) * HD].astype(BF16)


def queries(place, blocks, w_query):
    rows = blocks[0].shape[0]
    out = jax.ShapeDtypeStruct((2 * rows, HD), BF16)
    return pl.pallas_call(
        query_kernel,
        out_shape=(out, out),
        in_specs=smem(1) + vmem(2) + hbm(1),
        out_specs=tuple(vmem(2)),
        scratch_shapes=[
            pltpu.VMEM((4096, 512), BF16),
            pltpu.VMEM((2 * rows, 512), F32),
            pltpu.SemaphoreType.DMA((4,)),
        ],
        compiler_params=params(48),
        cost_estimate=pl.CostEstimate(
            flops=4 * rows * 4096 * 512, bytes_accessed=8 * MIB, transcendentals=0
        ),
        name="queries",
    )(place, *blocks, w_query)


def attend_kernel(pieces, keys, place, own_span, low_span, key_span, *refs):
    ids_own, ids_low, key_ids, near, far_low, near_low, far = refs[:7]
    arrays, outs, (query, ids, scores, peak, total, context) = refs[7:-10], refs[-10:-6], refs[-6:]
    block = ATTEND_ROWS
    scale = HD ** (-0.5) * math.log2(math.e)
    low, mp, z = place[1], place[2], place[7]

    for at, rows in enumerate((near, far_low, near_low, far)):
        query[at * 256 : (at + 1) * 256] = rows[...]
    for at, held in enumerate((ids_own, ids_low)):
        for flip in range(4):
            first = at * block + flip * 128
            row = held[pl.ds(jnp.bitwise_xor(mp, flip), 1)]
            ids[first : first + 128] = jnp.transpose(jnp.broadcast_to(row, (128, 128)))

    def one_block(at, _):
        rows = pl.ds(pl.multiple_of(at * block, block), block)
        lowest = jnp.where(at == 0, own_span[0, 0], low_span[0, 0])
        highest_id = jnp.where(at == 0, own_span[3, 127], low_span[3, 127])
        peak[...] = jnp.full_like(peak, -1e30)
        total[...] = jnp.zeros_like(total)
        context[...] = jnp.zeros_like(context)

        def rows_of(held):
            array, lead, row = held
            return arrays[array].at[lead + (pl.ds(row, keys),)]

        def for_each_part(step):
            for part, (flip_low, turn, row, piece_keys, piece_values) in enumerate(pieces):
                first = (jnp.bitwise_xor(low, flip_low) * 4 + (z + turn) % 4) * 512 + row
                meets = (key_span[0, first] <= highest_id) & (key_span[0, first + keys - 1] >= lowest)
                pl.when(meets)(
                    functools.partial(step, part, rows_of(piece_keys), rows_of(piece_values), first)
                )

        def score(part, part_keys, part_values, first):
            product = lax.dot_general(
                query[rows], part_keys[...], (((1,), (1,)), ((), ())), preferred_element_type=F32
            )
            own_ids = ids[rows]
            highest = peak[...]
            for lane in range(0, keys, 128):
                lane_ids = key_ids[:, pl.ds(pl.multiple_of(first + lane, 128), 128)]
                kept = jnp.where(own_ids == lane_ids, product[:, lane : lane + 128] * scale, -1e30)
                scores[part, :, lane : lane + 128] = kept
                highest = jnp.maximum(highest, kept)
            peak[...] = highest

        for_each_part(score)
        highest = jnp.max(peak[...], axis=-1, keepdims=True)

        def weigh(part, part_keys, part_values, first):
            weights = jnp.exp2(scores[part] - highest)
            sums = total[...]
            for lane in range(0, keys, 128):
                sums = sums + weights[:, lane : lane + 128]
            total[...] = sums
            context[...] += dot(weights.astype(BF16), part_values[...])

        for_each_part(weigh)
        whole = jnp.sum(total[...], axis=-1, keepdims=True)
        context[...] = context[...] / whole

        for tile in range(2):

            @pl.when(at == tile)
            def _():
                outs[2 * tile][...] = context[0:256].astype(BF16)
                outs[2 * tile + 1][...] = context[256:512].astype(BF16)

        return 0

    lax.fori_loop(0, 2, one_block, 0)


def attend(keys, pieces, arrays, place, ids_own, ids_low, key_ids, blocks):
    out = jax.ShapeDtypeStruct((256, HD), BF16)
    return pl.pallas_call(
        functools.partial(attend_kernel, pieces, keys),
        out_shape=(out,) * 4,
        in_specs=smem(4) + vmem(7 + len(arrays)),
        out_specs=tuple(vmem(4)),
        scratch_shapes=[
            pltpu.VMEM((2 * ATTEND_ROWS, HD), BF16),
            pltpu.VMEM((2 * ATTEND_ROWS, 128), jnp.int32),
            pltpu.VMEM((len(pieces), ATTEND_ROWS, keys), F32),
            pltpu.VMEM((ATTEND_ROWS, 128), F32),
            pltpu.VMEM((ATTEND_ROWS, 128), F32),
            pltpu.VMEM((ATTEND_ROWS, HD), F32),
        ],
        compiler_params=params(28),
        cost_estimate=pl.CostEstimate(
            flops=4 * 1024 * 4096 * 256, bytes_accessed=6 * MIB, transcendentals=1024 * 1024
        ),
        name="attend",
    )(place, ids_own, ids_low, key_ids, ids_own, ids_low, key_ids, *blocks, *arrays)


def output_kernel(first, place, c0, c1, c2, c3, w_own, *refs):
    pieces, (out, weight, arrived) = refs[:-3], refs[-3:]
    low, z, width = place[1], place[7], weight.shape[3]
    steps = out.shape[1] // width
    copies = []
    for step in range(steps):
        columns = pl.ds(first + step * width, width)
        moves = [(w_own.at[:, columns], weight.at[step, 0])]
        for head, row, turn, count, at in W_PIECES:
            start = jnp.bitwise_xor(low, head) * HD + (z + turn) % 4 * 64 + row
            target = weight.at[step, 1, pl.ds(pl.multiple_of(start, 32), count)]
            moves.append((pieces[at].at[:, columns], target))
        copies.append(
            [
                pltpu.make_async_copy(source, target, arrived.at[step, at])
                for at, (source, target) in enumerate(moves)
            ]
        )
    for moves in copies:
        for copy in moves:
            copy.start()
    near = jnp.where(low == 0, jnp.concatenate([c0[...], c2[...]], 1), jnp.concatenate([c2[...], c0[...]], 1))
    far = jnp.where(low == 0, jnp.concatenate([c1[...], c3[...]], 1), jnp.concatenate([c3[...], c1[...]], 1))
    for step, moves in enumerate(copies):
        for copy in moves:
            copy.wait()
        summed = dot(near, weight[step, 0]) + dot(far, weight[step, 1])
        out[:, step * width : (step + 1) * width] = summed.astype(out.dtype)


def outputs(place, contexts, w_own, pieces, part, parts):
    width, step = 4096 // parts, 512
    return pl.pallas_call(
        functools.partial(output_kernel, part * width),
        out_shape=jax.ShapeDtypeStruct((256, width), BF16),
        in_specs=smem(1) + vmem(4) + hbm(1 + len(pieces)),
        out_specs=vmem(1)[0],
        scratch_shapes=[
            pltpu.VMEM((width // step, 2, 512, step), BF16),
            pltpu.SemaphoreType.DMA((width // step, 1 + len(pieces))),
        ],
        compiler_params=params(48),
        cost_estimate=pl.CostEstimate(
            flops=2 * 256 * width * 1024, bytes_accessed=width * 2048, transcendentals=0
        ),
        name="outputs",
    )(place, *contexts, w_own, *pieces)


def per_device(
    decoder_rows,
    encoder_panel,
    norm_gain,
    w_query,
    w_key,
    w_value,
    w_output,
    decoder_segments,
    encoder_segments,
):
    section = lax.axis_index("section")
    seq = lax.axis_index("seq")
    mp = lax.axis_index("mp")
    low, z = seq // 4, seq % 4
    place = jnp.stack([section, low, mp] + [(section + offset) % 4 for offset in X_ORDER] + [z]).astype(
        jnp.int32
    )

    ids_own = decoder_segments[0].reshape(4, 128)

    def panel_of(offset, first, count):
        return lax.dynamic_slice(
            encoder_panel, ((section + offset) % 4, first, 0), (1, count, 256)
        )

    w_own = w_output[0]

    def rows_for_cut(head, turn):
        return lax.dynamic_slice(w_own, (head * HD + (z + turn) % 4 * 64, 0), (64, 4096))

    first, encoder_panel = lax.optimization_barrier((rows_for_cut(1 - low, 0), encoder_panel))
    piece = send(first, Y_CUT)
    own = panel_of(0, 0, 512)
    up, down = send(panel_of(1, 0, 512), X_UP), send(panel_of(3, 0, 512), X_DOWN)
    two = send(panel_of(2, 0, 512), X_TWO)
    local_rows = decoder_rows[0]
    hidden = normed_rows(local_rows, norm_gain[0])
    up, down, two, own_far, hidden, piece, w_own = lax.optimization_barrier(
        (up, down, two, send(own, Y_FAR), hidden, piece, w_own)
    )
    rest = jnp.concatenate([up, down, two])
    piece_below, piece_above = send(piece, Z_UP), send(piece, Z_DOWN)

    near_mine, near_other = queries(place, (hidden, send(hidden, CORE)), w_query[0])
    blocks = [own, send(own, CORE), own_far, send(own_far, CORE)]
    sums = key_values(place, blocks, w_key[0], w_value[0], ((0, 0, 0),))
    piece_below, piece_above, near_mine, near_other = lax.optimization_barrier(
        (piece_below, piece_above, near_mine, near_other)
    )
    far_rows = [piece, piece_below, piece_above]
    far_rows += [send(piece_below[:32], Z_UP), send(piece_above[32:], Z_DOWN)]
    cut_1, cut_2 = rows_for_cut(low, 1), rows_for_cut(low, 2)
    rest_far, ids_low, sums, near_mine, near_other, cut_1, cut_2, *far_rows = (
        lax.optimization_barrier(
            (
                send(rest, Y_FAR),
                send(ids_own, Y_LOW),
                sums,
                near_mine,
                near_other,
                cut_1,
                cut_2,
                *far_rows,
            )
        )
    )

    blocks = [rest, send(rest, CORE), rest_far, send(rest_far, CORE)]
    steps = ((1, 0, 1), (1, 1, 2), (1, 2, 3))
    mine, other = key_values(place, blocks, w_key[0], w_value[0], steps, (sums,))

    hidden, _ = lax.optimization_barrier((hidden, rest_far))
    hidden_cut = send(hidden, Y_CUT)
    below_0, above_0 = send(mine, Z_UP), send(mine, Z_DOWN)
    theirs, below_0, above_0, hidden_cut, piece, cut_1 = lax.optimization_barrier(
        (send(other, Y_LOW), below_0, above_0, hidden_cut, far_rows[0], cut_1)
    )
    below_1, above_1 = send(theirs, Z_UP), send(theirs, Z_DOWN)

    far_mine, far_other = queries(place, (hidden_cut, send(hidden_cut, CORE)), w_query[0])
    other_0, other_1 = send(piece, Y_LOW), send(cut_1, Y_CUT)
    below_1, above_1, far_mine, far_other, other_0, other_1, piece, cut_2 = (
        lax.optimization_barrier(
            (below_1, above_1, far_mine, far_other, other_0, other_1, far_rows[1], cut_2)
        )
    )
    across_keys = send(jnp.concatenate([below_0[0], below_1[0]]), Z_UP)
    across_values = send(jnp.concatenate([above_0[1], above_1[1]]), Z_DOWN)
    far_rows += [other_0, send(piece, Y_LOW), other_1, send(cut_2, Y_CUT)]

    blocks = (near_mine, send(far_other, Y_LOW), send(near_other, Y_LOW), far_mine)

    arrays, pieces = [across_keys, across_values], []
    for flip_low, (held, below, above) in enumerate(
        ((mine, below_0, above_0), (theirs, below_1, above_1))
    ):
        for turn, whole in ((0, held), (3, below), (1, above)):
            at = len(arrays)
            arrays.append(whole)
            for row in range(0, 512, KEYS):
                pieces.append((flip_low, turn, row, (at, (0,), row), (at, (1,), row)))
        for row in range(0, 512, KEYS):
            held_row = flip_low * 512 + row
            pieces.append((flip_low, 2, row, (0, (), held_row), (1, (), held_row)))

    contexts = attend(
        KEYS, pieces, arrays, place, ids_own, ids_low, encoder_segments, blocks
    )

    contexts = (contexts[0],) + tuple(
        send(context, pairs) for context, pairs in zip(contexts[1:], (Y_FAR, Y_LOW, Y_CUT))
    )
    summed = []
    for part in range(2):
        both = outputs(place, contexts, w_own, far_rows, part, 2)
        summed.append(both[:128].astype(F32) + send(both[128:], CORE).astype(F32))
    return (jnp.concatenate(summed, axis=1) + local_rows.astype(F32)).astype(BF16)[None]


def solution(mesh):
    in_specs = (
        P("section", ("seq", "mp"), None),
        P(None, "seq", ("section", "mp")),
        P("section", None),
        P("section", None, "mp"),
        P("section", None, "mp"),
        P("section", None, "mp"),
        P("section", "mp", None),
        P("section", "seq"),
        P("section", None),
    )
    out_specs = P("section", ("seq", "mp"), None)
    return jax.shard_map(
        per_device, mesh=mesh, in_specs=in_specs, out_specs=out_specs, check_vma=False
    )
```

```python
import functools
import math

import jax
import jax.numpy as jnp
from jax import lax
from jax.experimental import pallas as pl
from jax.experimental.pallas import tpu as pltpu
from jax.sharding import PartitionSpec as P

HD = 256
AXES = ("section", "seq", "mp")
SHAPE = (4, 2, 4, 2, 2)
KEYS = 256
ATTEND_ROWS = 512
MIB = 1 << 20
F32 = jnp.float32
BF16 = jnp.bfloat16


def route(target):
    pairs = []
    for source in range(math.prod(SHAPE)):
        at, rest = [], source
        for size in reversed(SHAPE):
            at.append(rest % size)
            rest //= size
        there = 0
        for place, size in zip(target(*reversed(at)), SHAPE):
            there = there * size + place % size
        pairs.append((source, there))
    return pairs


CORE = route(lambda x, l, z, h, c: (x, l, z, h, c + 1))
Y_FAR = route(lambda x, l, z, h, c: (x, l, z, h + 1, c))
Y_CUT = route(lambda x, l, z, h, c: (x, l + 1, z, h + 1, c))
Y_LOW_CORE = route(lambda x, l, z, h, c: (x, l + 1, z, h, c + 1))
Y_LOW = route(lambda x, l, z, h, c: (x, l + 1, z, h, c))
Z_UP = route(lambda x, l, z, h, c: (x, l, z + 1, h, c))
Z_DOWN = route(lambda x, l, z, h, c: (x, l, z - 1, h, c))
X_UP = route(lambda x, l, z, h, c: (x + 1, l, z, h, c))
X_DOWN = route(lambda x, l, z, h, c: (x - 1, l, z, h, c))
X_TWO = route(lambda x, l, z, h, c: (x + 2, l, z, h, c))
X_ORDER = (0, -1, 1, 2)
W_PIECES = (
    (0, 0, 0, 64, 0),
    (0, 0, 3, 64, 1),
    (0, 0, 1, 64, 2),
    (0, 0, 2, 32, 3),
    (0, 32, 2, 32, 4),
    (1, 0, 0, 64, 5),
    (1, 0, 3, 64, 6),
    (1, 0, 1, 64, 7),
    (1, 0, 2, 64, 8),
)
X_GROUPS = ((0,), (1, 2), (3,))


def send(array, pairs):
    return lax.ppermute(array, AXES, pairs)


def vmem(count):
    return [pl.BlockSpec(memory_space=pltpu.VMEM)] * count


def smem(count):
    return [pl.BlockSpec(memory_space=pltpu.SMEM)] * count


def params(mib):
    return pltpu.CompilerParams(vmem_limit_bytes=mib * MIB)


def normed_rows(layer_rows, gain):
    widened = layer_rows.astype(F32)
    mean_square = jnp.mean(widened * widened, axis=-1, keepdims=True)
    return (widened * lax.rsqrt(mean_square + 1e-06) * gain.astype(F32)).astype(BF16)


def dot(a, b):
    return jnp.dot(a, b, preferred_element_type=F32)


def fetch(source, held, arrived, pieces, piece):
    copies = [
        pltpu.make_async_copy(source.at[piece(at)], held.at[piece(at)], arrived.at[at])
        for at in range(pieces)
    ]
    for copy in copies:
        copy.start()
    return lambda at: copies[at].wait()


def row_piece(at):
    return (pl.ds(at * 1024, 1024),)


def key_value_kernel(steps, place, *refs):
    count = 4 * len(set(group for group, _, _ in steps))
    blocks, refs = refs[:count], refs[count:]
    w_key, w_value, refs = refs[0], refs[1], refs[2:]
    sums, refs = (None, refs) if steps[0][2] == 0 else (refs[0], refs[1:])
    keys, values, arrived = refs[-3:]
    copies = []
    for at, (_, _, step) in enumerate(steps):
        for flip in range(4):
            row = place[3 + step] * 1024 + jnp.bitwise_xor(place[2], flip) * 256
            source = pl.ds(pl.multiple_of(row, 256), 256)
            target = pl.ds(at * 1024 + flip * 256, 256)
            for which, (weight, held) in enumerate(((w_key, keys), (w_value, values))):
                copies.append(
                    pltpu.make_async_copy(
                        weight.at[source], held.at[target], arrived.at[which, at * 4 + flip]
                    )
                )
    for copy in copies:
        copy.start()
    if sums is None:
        total = refs[0]
    else:
        mine, other, total = refs[:3]
        total[...] = sums[...]
    first = min(group for group, _, _ in steps)
    for at, (group, lead, step) in enumerate(steps):
        panel = jnp.concatenate(
            [blocks[(group - first) * 4 + flip][lead] for flip in range(4)], axis=1
        )
        for copy in copies[at * 8 : at * 8 + 8]:
            copy.wait()
        for which, held in enumerate((keys, values)):
            for side in range(2):
                columns = slice(side * HD, (side + 1) * HD)
                product = dot(panel, held[at * 1024 : (at + 1) * 1024, columns])
                if step == 0:
                    total[which, :, columns] = product
                else:
                    total[which, :, columns] += product
    if sums is not None:
        for side in range(2):

            @pl.when(place[1] == side)
            def _():
                mine[...] = total[:, :, side * HD : (side + 1) * HD].astype(BF16)
                other[...] = total[:, :, (1 - side) * HD : (2 - side) * HD].astype(BF16)


def hbm(count):
    return [pl.BlockSpec(memory_space=pltpu.HBM)] * count


def key_values(place, blocks, w_key, w_value, steps, sums=()):
    rows = blocks[0].shape[1]
    total = (2, rows, 512)
    out = jax.ShapeDtypeStruct((2, rows, HD), BF16)
    depth = 1024 * len(steps)
    return pl.pallas_call(
        functools.partial(key_value_kernel, steps),
        out_shape=(out, out) if sums else jax.ShapeDtypeStruct(total, F32),
        in_specs=smem(1) + vmem(len(blocks)) + hbm(2) + vmem(len(sums)),
        out_specs=tuple(vmem(2)) if sums else vmem(1)[0],
        scratch_shapes=([pltpu.VMEM(total, F32)] if sums else [])
        + [
            pltpu.VMEM((depth, 512), BF16),
            pltpu.VMEM((depth, 512), BF16),
            pltpu.SemaphoreType.DMA((2, 4 * len(steps))),
        ],
        compiler_params=params(48),
        cost_estimate=pl.CostEstimate(
            flops=2 * rows * depth * 1024, bytes_accessed=depth * 3072, transcendentals=0
        ),
        name="key_values",
    )(place, *blocks, w_key, w_value, *sums)


def query_kernel(place, h0, h1, w_query, mine, other, weight, sums, arrived):
    wait = fetch(w_query, weight, arrived, 4, row_piece)
    for step in range(4):
        span = slice(step * 1024, (step + 1) * 1024)
        rows = jnp.concatenate([h0[:, span], h1[:, span]])
        wait(step)
        for side in range(2):
            columns = slice(side * HD, (side + 1) * HD)
            product = dot(rows, weight[span, columns])
            if step == 0:
                sums[:, columns] = product
            else:
                sums[:, columns] += product
    for side in range(2):

        @pl.when(place[1] == side)
        def _():
            mine[...] = sums[:, side * HD : (side + 1) * HD].astype(BF16)
            other[...] = sums[:, (1 - side) * HD : (2 - side) * HD].astype(BF16)


def queries(place, blocks, w_query):
    rows = blocks[0].shape[0]
    out = jax.ShapeDtypeStruct((2 * rows, HD), BF16)
    return pl.pallas_call(
        query_kernel,
        out_shape=(out, out),
        in_specs=smem(1) + vmem(2) + hbm(1),
        out_specs=tuple(vmem(2)),
        scratch_shapes=[
            pltpu.VMEM((4096, 512), BF16),
            pltpu.VMEM((2 * rows, 512), F32),
            pltpu.SemaphoreType.DMA((4,)),
        ],
        compiler_params=params(48),
        cost_estimate=pl.CostEstimate(
            flops=4 * rows * 4096 * 512, bytes_accessed=8 * MIB, transcendentals=0
        ),
        name="queries",
    )(place, *blocks, w_query)


def attend_kernel(pieces, keys, last, place, own_span, low_span, key_span, *refs):
    ids_own, ids_low, key_ids, near, far_low, near_low, far = refs[:7]
    query, ids, scores, peak, total, context = refs[-6:]
    outs, refs = (refs[-10:-6], refs[7:-10]) if last else (refs[-9:-6], refs[7:-9])
    arrays, before = (refs[:-3], refs[-3:]) if last else (refs, None)
    block = ATTEND_ROWS
    scale = HD ** (-0.5) * math.log2(math.e)
    low, mp, z = place[1], place[2], place[7]

    for at, rows in enumerate((near, far_low, near_low, far)):
        query[at * 256 : (at + 1) * 256] = rows[...]
    for at, held in enumerate((ids_own, ids_low)):
        for flip in range(4):
            first = at * block + flip * 128
            row = held[pl.ds(jnp.bitwise_xor(mp, flip), 1)]
            ids[first : first + 128] = jnp.transpose(jnp.broadcast_to(row, (128, 128)))

    def one_block(at, _):
        rows = pl.ds(pl.multiple_of(at * block, block), block)
        lowest = jnp.where(at == 0, own_span[0, 0], low_span[0, 0])
        highest_id = jnp.where(at == 0, own_span[3, 127], low_span[3, 127])
        if last:
            peak[...] = before[0][rows]
            earlier = jnp.max(peak[...], axis=-1, keepdims=True)
        else:
            peak[...] = jnp.full_like(peak, -1e30)
            total[...] = jnp.zeros_like(total)
            context[...] = jnp.zeros_like(context)

        def rows_of(held):
            array, lead, row = held
            return arrays[array].at[lead + (pl.ds(row, keys),)]

        def for_each_part(step):
            for part, (flip_low, turn, row, piece_keys, piece_values) in enumerate(pieces):
                first = (jnp.bitwise_xor(low, flip_low) * 4 + (z + turn) % 4) * 512 + row
                meets = (key_span[0, first] <= highest_id) & (key_span[0, first + keys - 1] >= lowest)
                pl.when(meets)(
                    functools.partial(step, part, rows_of(piece_keys), rows_of(piece_values), first)
                )

        def score(part, part_keys, part_values, first):
            product = lax.dot_general(
                query[rows], part_keys[...], (((1,), (1,)), ((), ())), preferred_element_type=F32
            )
            own_ids = ids[rows]
            highest = peak[...]
            for lane in range(0, keys, 128):
                lane_ids = key_ids[:, pl.ds(pl.multiple_of(first + lane, 128), 128)]
                kept = jnp.where(own_ids == lane_ids, product[:, lane : lane + 128] * scale, -1e30)
                scores[part, :, lane : lane + 128] = kept
                highest = jnp.maximum(highest, kept)
            peak[...] = highest

        for_each_part(score)
        highest = jnp.max(peak[...], axis=-1, keepdims=True)
        if last:
            shrink = jnp.exp2(earlier - highest)
            total[...] = before[1][rows] * shrink
            context[...] = before[2][rows] * shrink

        def weigh(part, part_keys, part_values, first):
            weights = jnp.exp2(scores[part] - highest)
            sums = total[...]
            for lane in range(0, keys, 128):
                sums = sums + weights[:, lane : lane + 128]
            total[...] = sums
            context[...] += dot(weights.astype(BF16), part_values[...])

        for_each_part(weigh)
        if not last:
            for out, value in zip(outs, (peak, total, context)):
                out[rows] = value[...]
            return 0

        whole = jnp.sum(total[...], axis=-1, keepdims=True)
        context[...] = context[...] / whole

        for tile in range(2):

            @pl.when(at == tile)
            def _():
                outs[2 * tile][...] = context[0:256].astype(BF16)
                outs[2 * tile + 1][...] = context[256:512].astype(BF16)

        return 0

    lax.fori_loop(0, 2, one_block, 0)


def attend(keys, pieces, arrays, place, ids_own, ids_low, key_ids, blocks, before=()):
    rows = 2 * ATTEND_ROWS
    context = jax.ShapeDtypeStruct((256, HD), BF16)
    state = [jax.ShapeDtypeStruct((rows, width), F32) for width in (128, 128, HD)]
    outs = (context,) * 4 if before else tuple(state)
    return pl.pallas_call(
        functools.partial(attend_kernel, pieces, keys, bool(before)),
        out_shape=outs,
        in_specs=smem(4) + vmem(7 + len(arrays) + len(before)),
        out_specs=tuple(vmem(len(outs))),
        scratch_shapes=[
            pltpu.VMEM((rows, HD), BF16),
            pltpu.VMEM((rows, 128), jnp.int32),
            pltpu.VMEM((len(pieces), ATTEND_ROWS, keys), F32),
            pltpu.VMEM((ATTEND_ROWS, 128), F32),
            pltpu.VMEM((ATTEND_ROWS, 128), F32),
            pltpu.VMEM((ATTEND_ROWS, HD), F32),
        ],
        compiler_params=params(28),
        cost_estimate=pl.CostEstimate(
            flops=256 * 1024 * 256 * len(pieces),
            bytes_accessed=6 * MIB,
            transcendentals=1024 * 64 * len(pieces),
        ),
        name="attend",
    )(place, ids_own, ids_low, key_ids, ids_own, ids_low, key_ids, *blocks, *arrays, *before)


def output_kernel(first, place, c0, c1, c2, c3, w_own, *refs):
    pieces, (out, weight, arrived) = refs[:-3], refs[-3:]
    low, z, width = place[1], place[7], weight.shape[3]
    steps = out.shape[1] // width
    copies = []
    for step in range(steps):
        columns = pl.ds(first + step * width, width)
        moves = [(w_own.at[:, columns], weight.at[step, 0])]
        for head, row, turn, count, at in W_PIECES:
            start = jnp.bitwise_xor(low, head) * HD + (z + turn) % 4 * 64 + row
            target = weight.at[step, 1, pl.ds(pl.multiple_of(start, 32), count)]
            moves.append((pieces[at].at[:, columns], target))
        copies.append(
            [
                pltpu.make_async_copy(source, target, arrived.at[step, at])
                for at, (source, target) in enumerate(moves)
            ]
        )
    for moves in copies:
        for copy in moves:
            copy.start()
    near = jnp.where(low == 0, jnp.concatenate([c0[...], c2[...]], 1), jnp.concatenate([c2[...], c0[...]], 1))
    far = jnp.where(low == 0, jnp.concatenate([c1[...], c3[...]], 1), jnp.concatenate([c3[...], c1[...]], 1))
    for step, moves in enumerate(copies):
        for copy in moves:
            copy.wait()
        summed = dot(near, weight[step, 0]) + dot(far, weight[step, 1])
        out[:, step * width : (step + 1) * width] = summed.astype(out.dtype)


def outputs(place, contexts, w_own, pieces, part, parts):
    width, step = 4096 // parts, 1024
    return pl.pallas_call(
        functools.partial(output_kernel, part * width),
        out_shape=jax.ShapeDtypeStruct((256, width), BF16),
        in_specs=smem(1) + vmem(4) + hbm(1 + len(pieces)),
        out_specs=vmem(1)[0],
        scratch_shapes=[
            pltpu.VMEM((width // step, 2, 512, step), BF16),
            pltpu.SemaphoreType.DMA((width // step, 1 + len(pieces))),
        ],
        compiler_params=params(48),
        cost_estimate=pl.CostEstimate(
            flops=2 * 256 * width * 1024, bytes_accessed=width * 2048, transcendentals=0
        ),
        name="outputs",
    )(place, *contexts, w_own, *pieces)


def per_device(
    decoder_rows,
    encoder_panel,
    norm_gain,
    w_query,
    w_key,
    w_value,
    w_output,
    decoder_segments,
    encoder_segments,
):
    section = lax.axis_index("section")
    seq = lax.axis_index("seq")
    mp = lax.axis_index("mp")
    low, z = seq // 4, seq % 4
    place = jnp.stack([section, low, mp] + [(section + offset) % 4 for offset in X_ORDER] + [z]).astype(
        jnp.int32
    )

    ids_own = decoder_segments[0].reshape(4, 128)

    def panel_of(offset, first, count):
        return lax.dynamic_slice(
            encoder_panel, ((section + offset) % 4, first, 0), (1, count, 256)
        )

    w_own = w_output[0]

    def rows_for_cut(head, turn):
        return lax.dynamic_slice(w_own, (head * HD + (z + turn) % 4 * 64, 0), (64, 4096))

    first, encoder_panel = lax.optimization_barrier((rows_for_cut(1 - low, 0), encoder_panel))
    piece = send(first, Y_CUT)
    own = panel_of(0, 0, 512)
    up, down = send(panel_of(1, 0, 512), X_UP), send(panel_of(3, 0, 512), X_DOWN)
    two = send(panel_of(2, 0, 512), X_TWO)
    local_rows = decoder_rows[0]
    hidden = normed_rows(local_rows, norm_gain[0])
    up, down, two, own_far, hidden, piece, w_own = lax.optimization_barrier(
        (up, down, two, send(own, Y_FAR), hidden, piece, w_own)
    )
    rest = jnp.concatenate([up, down, two])
    piece_below, piece_above = send(piece, Z_UP), send(piece, Z_DOWN)

    near_mine, near_other = queries(place, (hidden, send(hidden, CORE)), w_query[0])
    blocks = [own, send(own, CORE), own_far, send(own_far, CORE)]
    sums = key_values(place, blocks, w_key[0], w_value[0], ((0, 0, 0),))
    piece_below, piece_above, near_mine, near_other = lax.optimization_barrier(
        (piece_below, piece_above, near_mine, near_other)
    )
    far_rows = [piece, piece_below, piece_above]
    far_rows += [send(piece_below[:32], Z_UP), send(piece_above[32:], Z_DOWN)]
    cut_1, cut_2 = rows_for_cut(low, 1), rows_for_cut(low, 2)
    rest_far, ids_low, sums, near_mine, near_other, cut_1, cut_2, *far_rows = (
        lax.optimization_barrier(
            (
                send(rest, Y_FAR),
                send(ids_own, Y_LOW),
                sums,
                near_mine,
                near_other,
                cut_1,
                cut_2,
                *far_rows,
            )
        )
    )

    blocks = [rest, send(rest, CORE), rest_far, send(rest_far, CORE)]
    steps = ((1, 0, 1), (1, 1, 2), (1, 2, 3))
    mine, other = key_values(place, blocks, w_key[0], w_value[0], steps, (sums,))

    hidden, _ = lax.optimization_barrier((hidden, rest_far))
    hidden_cut = send(hidden, Y_CUT)
    below_0, above_0 = send(mine, Z_UP), send(mine, Z_DOWN)
    theirs, below_0, above_0, hidden_cut, piece, cut_1, near_low = lax.optimization_barrier(
        (
            send(other, Y_LOW),
            below_0,
            above_0,
            hidden_cut,
            far_rows[0],
            cut_1,
            send(near_other, Y_LOW),
        )
    )
    below_1, above_1 = send(theirs, Z_UP), send(theirs, Z_DOWN)

    far_mine, far_other = queries(place, (hidden_cut, send(hidden_cut, CORE)), w_query[0])
    other_0, other_1 = send(piece, Y_LOW), send(cut_1, Y_CUT)
    far_low = send(far_other, Y_LOW)
    below_1, above_1, far_mine, far_low, other_0, other_1, piece, cut_2 = (
        lax.optimization_barrier(
            (below_1, above_1, far_mine, far_low, other_0, other_1, far_rows[1], cut_2)
        )
    )
    across_keys = send(jnp.concatenate([below_0[0], below_1[0]]), Z_UP)
    across_values = send(jnp.concatenate([above_0[1], above_1[1]]), Z_DOWN)
    far_rows += [other_0, send(piece, Y_LOW), other_1, send(cut_2, Y_CUT)]

    blocks = (near_mine, far_low, near_low, far_mine)

    arrays, pieces, last_pieces = [], [], []
    for flip_low, (held, below, above) in enumerate(
        ((mine, below_0, above_0), (theirs, below_1, above_1))
    ):
        for turn, whole in ((0, held), (3, below), (1, above)):
            at = len(arrays)
            arrays.append(whole)
            for row in range(0, 512, KEYS):
                pieces.append((flip_low, turn, row, (at, (0,), row), (at, (1,), row)))
        for row in range(0, 512, KEYS):
            held_row = flip_low * 512 + row
            last_pieces.append((flip_low, 2, row, (0, (), held_row), (1, (), held_row)))

    state = attend(KEYS, pieces, arrays, place, ids_own, ids_low, encoder_segments, blocks)
    arrays = [across_keys, across_values]
    contexts = attend(
        KEYS, last_pieces, arrays, place, ids_own, ids_low, encoder_segments, blocks, state
    )

    contexts = (contexts[0],) + tuple(
        send(context, pairs) for context, pairs in zip(contexts[1:], (Y_FAR, Y_LOW, Y_CUT))
    )
    summed = []
    for part in range(2):
        both = outputs(place, contexts, w_own, far_rows, part, 2)
        summed.append(both[:128].astype(F32) + send(both[128:], CORE).astype(F32))
    return (jnp.concatenate(summed, axis=1) + local_rows.astype(F32)).astype(BF16)[None]


def solution(mesh):
    in_specs = (
        P("section", ("seq", "mp"), None),
        P(None, "seq", ("section", "mp")),
        P("section", None),
        P("section", None, "mp"),
        P("section", None, "mp"),
        P("section", None, "mp"),
        P("section", "mp", None),
        P("section", "seq"),
        P("section", None),
    )
    out_specs = P("section", ("seq", "mp"), None)
    return jax.shard_map(
        per_device, mesh=mesh, in_specs=in_specs, out_specs=out_specs, check_vma=False
    )
```

```python
import functools
import math

import jax
import jax.numpy as jnp
from jax import lax
from jax.experimental import pallas as pl
from jax.experimental.pallas import tpu as pltpu
from jax.sharding import PartitionSpec as P

HD = 256
AXES = ("section", "seq", "mp")
SHAPE = (4, 2, 4, 2, 2)
KEYS = 512
ATTEND_ROWS = 512
MIB = 1 << 20
F32 = jnp.float32
BF16 = jnp.bfloat16


def route(target):
    pairs = []
    for source in range(math.prod(SHAPE)):
        at, rest = [], source
        for size in reversed(SHAPE):
            at.append(rest % size)
            rest //= size
        there = 0
        for place, size in zip(target(*reversed(at)), SHAPE):
            there = there * size + place % size
        pairs.append((source, there))
    return pairs


CORE = route(lambda x, l, z, h, c: (x, l, z, h, c + 1))
Y_FAR = route(lambda x, l, z, h, c: (x, l, z, h + 1, c))
Y_CUT = route(lambda x, l, z, h, c: (x, l + 1, z, h + 1, c))
Y_LOW_CORE = route(lambda x, l, z, h, c: (x, l + 1, z, h, c + 1))
Y_LOW = route(lambda x, l, z, h, c: (x, l + 1, z, h, c))
Z_UP = route(lambda x, l, z, h, c: (x, l, z + 1, h, c))
Z_DOWN = route(lambda x, l, z, h, c: (x, l, z - 1, h, c))
X_UP = route(lambda x, l, z, h, c: (x + 1, l, z, h, c))
X_DOWN = route(lambda x, l, z, h, c: (x - 1, l, z, h, c))
X_TWO = route(lambda x, l, z, h, c: (x + 2, l, z, h, c))
X_ORDER = (0, -1, 1, 2)
W_PIECES = (
    (0, 0, 0, 64, 0),
    (0, 0, 3, 64, 1),
    (0, 0, 1, 64, 2),
    (0, 0, 2, 32, 3),
    (0, 32, 2, 32, 4),
    (1, 0, 0, 64, 5),
    (1, 0, 3, 64, 6),
    (1, 0, 1, 64, 7),
    (1, 0, 2, 64, 8),
)
X_GROUPS = ((0,), (1, 2), (3,))


def send(array, pairs):
    return lax.ppermute(array, AXES, pairs)


def vmem(count):
    return [pl.BlockSpec(memory_space=pltpu.VMEM)] * count


def smem(count):
    return [pl.BlockSpec(memory_space=pltpu.SMEM)] * count


def params(mib):
    return pltpu.CompilerParams(vmem_limit_bytes=mib * MIB)


def normed_rows(layer_rows, gain):
    widened = layer_rows.astype(F32)
    mean_square = jnp.mean(widened * widened, axis=-1, keepdims=True)
    return (widened * lax.rsqrt(mean_square + 1e-06) * gain.astype(F32)).astype(BF16)


def dot(a, b):
    return jnp.dot(a, b, preferred_element_type=F32)


def fetch(source, held, arrived, pieces, piece):
    copies = [
        pltpu.make_async_copy(source.at[piece(at)], held.at[piece(at)], arrived.at[at])
        for at in range(pieces)
    ]
    for copy in copies:
        copy.start()
    return lambda at: copies[at].wait()


def row_piece(at):
    return (pl.ds(at * 1024, 1024),)


def key_value_kernel(steps, place, *refs):
    count = 4 * len(set(group for group, _, _ in steps))
    blocks, refs = refs[:count], refs[count:]
    w_key, w_value, refs = refs[0], refs[1], refs[2:]
    sums, refs = (None, refs) if steps[0][2] == 0 else (refs[0], refs[1:])
    keys, values, arrived = refs[-3:]
    copies = []
    for at, (_, _, step) in enumerate(steps):
        for flip in range(4):
            row = place[3 + step] * 1024 + jnp.bitwise_xor(place[2], flip) * 256
            source = pl.ds(pl.multiple_of(row, 256), 256)
            target = pl.ds(at * 1024 + flip * 256, 256)
            for which, (weight, held) in enumerate(((w_key, keys), (w_value, values))):
                copies.append(
                    pltpu.make_async_copy(
                        weight.at[source], held.at[target], arrived.at[which, at * 4 + flip]
                    )
                )
    for copy in copies:
        copy.start()
    if sums is None:
        total = refs[0]
    else:
        mine, other, total = refs[:3]
        total[...] = sums[...]
    first = min(group for group, _, _ in steps)
    for at, (group, lead, step) in enumerate(steps):
        panel = jnp.concatenate(
            [blocks[(group - first) * 4 + flip][lead] for flip in range(4)], axis=1
        )
        for copy in copies[at * 8 : at * 8 + 8]:
            copy.wait()
        for which, held in enumerate((keys, values)):
            for side in range(2):
                columns = slice(side * HD, (side + 1) * HD)
                product = dot(panel, held[at * 1024 : (at + 1) * 1024, columns])
                if step == 0:
                    total[which, :, columns] = product
                else:
                    total[which, :, columns] += product
    if sums is not None:
        for side in range(2):

            @pl.when(place[1] == side)
            def _():
                mine[...] = total[:, :, side * HD : (side + 1) * HD].astype(BF16)
                other[...] = total[:, :, (1 - side) * HD : (2 - side) * HD].astype(BF16)


def hbm(count):
    return [pl.BlockSpec(memory_space=pltpu.HBM)] * count


def key_values(place, blocks, w_key, w_value, steps, sums=()):
    rows = blocks[0].shape[1]
    total = (2, rows, 512)
    out = jax.ShapeDtypeStruct((2, rows, HD), BF16)
    depth = 1024 * len(steps)
    return pl.pallas_call(
        functools.partial(key_value_kernel, steps),
        out_shape=(out, out) if sums else jax.ShapeDtypeStruct(total, F32),
        in_specs=smem(1) + vmem(len(blocks)) + hbm(2) + vmem(len(sums)),
        out_specs=tuple(vmem(2)) if sums else vmem(1)[0],
        scratch_shapes=([pltpu.VMEM(total, F32)] if sums else [])
        + [
            pltpu.VMEM((depth, 512), BF16),
            pltpu.VMEM((depth, 512), BF16),
            pltpu.SemaphoreType.DMA((2, 4 * len(steps))),
        ],
        compiler_params=params(48),
        cost_estimate=pl.CostEstimate(
            flops=2 * rows * depth * 1024, bytes_accessed=depth * 3072, transcendentals=0
        ),
        name="key_values",
    )(place, *blocks, w_key, w_value, *sums)


def query_kernel(place, h0, h1, w_query, mine, other, weight, sums, arrived):
    wait = fetch(w_query, weight, arrived, 4, row_piece)
    for step in range(4):
        span = slice(step * 1024, (step + 1) * 1024)
        rows = jnp.concatenate([h0[:, span], h1[:, span]])
        wait(step)
        for side in range(2):
            columns = slice(side * HD, (side + 1) * HD)
            product = dot(rows, weight[span, columns])
            if step == 0:
                sums[:, columns] = product
            else:
                sums[:, columns] += product
    for side in range(2):

        @pl.when(place[1] == side)
        def _():
            mine[...] = sums[:, side * HD : (side + 1) * HD].astype(BF16)
            other[...] = sums[:, (1 - side) * HD : (2 - side) * HD].astype(BF16)


def queries(place, blocks, w_query):
    rows = blocks[0].shape[0]
    out = jax.ShapeDtypeStruct((2 * rows, HD), BF16)
    return pl.pallas_call(
        query_kernel,
        out_shape=(out, out),
        in_specs=smem(1) + vmem(2) + hbm(1),
        out_specs=tuple(vmem(2)),
        scratch_shapes=[
            pltpu.VMEM((4096, 512), BF16),
            pltpu.VMEM((2 * rows, 512), F32),
            pltpu.SemaphoreType.DMA((4,)),
        ],
        compiler_params=params(48),
        cost_estimate=pl.CostEstimate(
            flops=4 * rows * 4096 * 512, bytes_accessed=8 * MIB, transcendentals=0
        ),
        name="queries",
    )(place, *blocks, w_query)


def attend_kernel(pieces, keys, last, place, own_span, low_span, key_span, *refs):
    ids_own, ids_low, key_ids, near, far_low, near_low, far = refs[:7]
    query, ids, scores, peak, total, context = refs[-6:]
    outs, refs = (refs[-10:-6], refs[7:-10]) if last else (refs[-9:-6], refs[7:-9])
    arrays, before = (refs[:-3], refs[-3:]) if last else (refs, None)
    block = ATTEND_ROWS
    scale = HD ** (-0.5) * math.log2(math.e)
    low, mp, z = place[1], place[2], place[7]

    for at, rows in enumerate((near, far_low, near_low, far)):
        query[at * 256 : (at + 1) * 256] = rows[...]
    for at, held in enumerate((ids_own, ids_low)):
        for flip in range(4):
            first = at * block + flip * 128
            row = held[pl.ds(jnp.bitwise_xor(mp, flip), 1)]
            ids[first : first + 128] = jnp.transpose(jnp.broadcast_to(row, (128, 128)))

    def one_block(at, _):
        rows = pl.ds(pl.multiple_of(at * block, block), block)
        lowest = jnp.where(at == 0, own_span[0, 0], low_span[0, 0])
        highest_id = jnp.where(at == 0, own_span[3, 127], low_span[3, 127])
        if last:
            peak[...] = before[0][rows]
            earlier = jnp.max(peak[...], axis=-1, keepdims=True)
        else:
            peak[...] = jnp.full_like(peak, -1e30)
            total[...] = jnp.zeros_like(total)
            context[...] = jnp.zeros_like(context)

        def rows_of(held):
            array, lead, row = held
            return arrays[array].at[lead + (pl.ds(row, keys),)]

        def for_each_part(step):
            for part, (flip_low, turn, row, piece_keys, piece_values) in enumerate(pieces):
                first = (jnp.bitwise_xor(low, flip_low) * 4 + (z + turn) % 4) * 512 + row
                meets = (key_span[0, first] <= highest_id) & (key_span[0, first + keys - 1] >= lowest)
                pl.when(meets)(
                    functools.partial(step, part, rows_of(piece_keys), rows_of(piece_values), first)
                )

        def score(part, part_keys, part_values, first):
            product = lax.dot_general(
                query[rows], part_keys[...], (((1,), (1,)), ((), ())), preferred_element_type=F32
            )
            own_ids = ids[rows]
            highest = peak[...]
            for lane in range(0, keys, 128):
                lane_ids = key_ids[:, pl.ds(pl.multiple_of(first + lane, 128), 128)]
                kept = jnp.where(own_ids == lane_ids, product[:, lane : lane + 128] * scale, -1e30)
                scores[part, :, lane : lane + 128] = kept
                highest = jnp.maximum(highest, kept)
            peak[...] = highest

        for_each_part(score)
        highest = jnp.max(peak[...], axis=-1, keepdims=True)
        if last:
            shrink = jnp.exp2(earlier - highest)
            total[...] = before[1][rows] * shrink
            context[...] = before[2][rows] * shrink

        def weigh(part, part_keys, part_values, first):
            weights = jnp.exp2(scores[part] - highest)
            sums = total[...]
            for lane in range(0, keys, 128):
                sums = sums + weights[:, lane : lane + 128]
            total[...] = sums
            context[...] += dot(weights.astype(BF16), part_values[...])

        for_each_part(weigh)
        if not last:
            for out, value in zip(outs, (peak, total, context)):
                out[rows] = value[...]
            return 0

        whole = jnp.sum(total[...], axis=-1, keepdims=True)
        context[...] = context[...] / whole

        for tile in range(2):

            @pl.when(at == tile)
            def _():
                outs[2 * tile][...] = context[0:256].astype(BF16)
                outs[2 * tile + 1][...] = context[256:512].astype(BF16)

        return 0

    lax.fori_loop(0, 2, one_block, 0)


def attend(keys, pieces, arrays, place, ids_own, ids_low, key_ids, blocks, before=()):
    rows = 2 * ATTEND_ROWS
    context = jax.ShapeDtypeStruct((256, HD), BF16)
    state = [jax.ShapeDtypeStruct((rows, width), F32) for width in (128, 128, HD)]
    outs = (context,) * 4 if before else tuple(state)
    return pl.pallas_call(
        functools.partial(attend_kernel, pieces, keys, bool(before)),
        out_shape=outs,
        in_specs=smem(4) + vmem(7 + len(arrays) + len(before)),
        out_specs=tuple(vmem(len(outs))),
        scratch_shapes=[
            pltpu.VMEM((rows, HD), BF16),
            pltpu.VMEM((rows, 128), jnp.int32),
            pltpu.VMEM((len(pieces), ATTEND_ROWS, keys), F32),
            pltpu.VMEM((ATTEND_ROWS, 128), F32),
            pltpu.VMEM((ATTEND_ROWS, 128), F32),
            pltpu.VMEM((ATTEND_ROWS, HD), F32),
        ],
        compiler_params=params(28),
        cost_estimate=pl.CostEstimate(
            flops=256 * 1024 * 256 * len(pieces),
            bytes_accessed=6 * MIB,
            transcendentals=1024 * 64 * len(pieces),
        ),
        name="attend",
    )(place, ids_own, ids_low, key_ids, ids_own, ids_low, key_ids, *blocks, *arrays, *before)


def output_kernel(first, place, c0, c1, c2, c3, w_own, *refs):
    pieces, (out, weight, arrived) = refs[:-3], refs[-3:]
    low, z, width = place[1], place[7], weight.shape[3]
    steps = out.shape[1] // width
    copies = []
    for step in range(steps):
        columns = pl.ds(first + step * width, width)
        moves = [(w_own.at[:, columns], weight.at[step, 0])]
        for head, row, turn, count, at in W_PIECES:
            start = jnp.bitwise_xor(low, head) * HD + (z + turn) % 4 * 64 + row
            target = weight.at[step, 1, pl.ds(pl.multiple_of(start, 32), count)]
            moves.append((pieces[at].at[:, columns], target))
        copies.append(
            [
                pltpu.make_async_copy(source, target, arrived.at[step, at])
                for at, (source, target) in enumerate(moves)
            ]
        )
    for moves in copies:
        for copy in moves:
            copy.start()
    near = jnp.where(low == 0, jnp.concatenate([c0[...], c2[...]], 1), jnp.concatenate([c2[...], c0[...]], 1))
    far = jnp.where(low == 0, jnp.concatenate([c1[...], c3[...]], 1), jnp.concatenate([c3[...], c1[...]], 1))
    for step, moves in enumerate(copies):
        for copy in moves:
            copy.wait()
        summed = dot(near, weight[step, 0]) + dot(far, weight[step, 1])
        out[:, step * width : (step + 1) * width] = summed.astype(out.dtype)


def outputs(place, contexts, w_own, pieces, part, parts):
    width, step = 4096 // parts, 1024
    return pl.pallas_call(
        functools.partial(output_kernel, part * width),
        out_shape=jax.ShapeDtypeStruct((256, width), BF16),
        in_specs=smem(1) + vmem(4) + hbm(1 + len(pieces)),
        out_specs=vmem(1)[0],
        scratch_shapes=[
            pltpu.VMEM((width // step, 2, 512, step), BF16),
            pltpu.SemaphoreType.DMA((width // step, 1 + len(pieces))),
        ],
        compiler_params=params(48),
        cost_estimate=pl.CostEstimate(
            flops=2 * 256 * width * 1024, bytes_accessed=width * 2048, transcendentals=0
        ),
        name="outputs",
    )(place, *contexts, w_own, *pieces)


def per_device(
    decoder_rows,
    encoder_panel,
    norm_gain,
    w_query,
    w_key,
    w_value,
    w_output,
    decoder_segments,
    encoder_segments,
):
    section = lax.axis_index("section")
    seq = lax.axis_index("seq")
    mp = lax.axis_index("mp")
    low, z = seq // 4, seq % 4
    place = jnp.stack([section, low, mp] + [(section + offset) % 4 for offset in X_ORDER] + [z]).astype(
        jnp.int32
    )

    ids_own = decoder_segments[0].reshape(4, 128)

    def panel_of(offset, first, count):
        return lax.dynamic_slice(
            encoder_panel, ((section + offset) % 4, first, 0), (1, count, 256)
        )

    w_own = w_output[0]

    def rows_for_cut(head, turn):
        return lax.dynamic_slice(w_own, (head * HD + (z + turn) % 4 * 64, 0), (64, 4096))

    first, encoder_panel = lax.optimization_barrier((rows_for_cut(1 - low, 0), encoder_panel))
    piece = send(first, Y_CUT)
    own = panel_of(0, 0, 512)
    up, down = send(panel_of(1, 0, 512), X_UP), send(panel_of(3, 0, 512), X_DOWN)
    two = send(panel_of(2, 0, 512), X_TWO)
    local_rows = decoder_rows[0]
    hidden = normed_rows(local_rows, norm_gain[0])
    up, down, two, own_far, hidden, piece, w_own = lax.optimization_barrier(
        (up, down, two, send(own, Y_FAR), hidden, piece, w_own)
    )
    rest = jnp.concatenate([up, down, two])
    piece_below, piece_above = send(piece, Z_UP), send(piece, Z_DOWN)

    near_mine, near_other = queries(place, (hidden, send(hidden, CORE)), w_query[0])
    blocks = [own, send(own, CORE), own_far, send(own_far, CORE)]
    sums = key_values(place, blocks, w_key[0], w_value[0], ((0, 0, 0),))
    piece_below, piece_above, near_mine, near_other = lax.optimization_barrier(
        (piece_below, piece_above, near_mine, near_other)
    )
    far_rows = [piece, piece_below, piece_above]
    far_rows += [send(piece_below[:32], Z_UP), send(piece_above[32:], Z_DOWN)]
    cut_1, cut_2 = rows_for_cut(low, 1), rows_for_cut(low, 2)
    rest_far, ids_low, sums, near_mine, near_other, cut_1, cut_2, *far_rows = (
        lax.optimization_barrier(
            (
                send(rest, Y_FAR),
                send(ids_own, Y_LOW),
                sums,
                near_mine,
                near_other,
                cut_1,
                cut_2,
                *far_rows,
            )
        )
    )

    blocks = [rest, send(rest, CORE), rest_far, send(rest_far, CORE)]
    steps = ((1, 0, 1), (1, 1, 2), (1, 2, 3))
    mine, other = key_values(place, blocks, w_key[0], w_value[0], steps, (sums,))

    hidden, _ = lax.optimization_barrier((hidden, rest_far))
    hidden_cut = send(hidden, Y_CUT)
    below_0, above_0 = send(mine, Z_UP), send(mine, Z_DOWN)
    theirs, below_0, above_0, hidden_cut, piece, cut_1, near_low = lax.optimization_barrier(
        (
            send(other, Y_LOW),
            below_0,
            above_0,
            hidden_cut,
            far_rows[0],
            cut_1,
            send(near_other, Y_LOW),
        )
    )
    below_1, above_1 = send(theirs, Z_UP), send(theirs, Z_DOWN)

    far_mine, far_other = queries(place, (hidden_cut, send(hidden_cut, CORE)), w_query[0])
    other_0, other_1 = send(piece, Y_LOW), send(cut_1, Y_CUT)
    far_low = send(far_other, Y_LOW)
    below_1, above_1, far_mine, far_low, other_0, other_1, piece, cut_2 = (
        lax.optimization_barrier(
            (below_1, above_1, far_mine, far_low, other_0, other_1, far_rows[1], cut_2)
        )
    )
    across_keys = send(jnp.concatenate([below_0[0], below_1[0]]), Z_UP)
    across_values = send(jnp.concatenate([above_0[1], above_1[1]]), Z_DOWN)
    far_rows += [other_0, send(piece, Y_LOW), other_1, send(cut_2, Y_CUT)]

    blocks = (near_mine, far_low, near_low, far_mine)

    arrays, pieces, last_pieces = [], [], []
    for flip_low, (held, below, above) in enumerate(
        ((mine, below_0, above_0), (theirs, below_1, above_1))
    ):
        for turn, whole in ((0, held), (3, below), (1, above)):
            at = len(arrays)
            arrays.append(whole)
            for row in range(0, 512, KEYS):
                pieces.append((flip_low, turn, row, (at, (0,), row), (at, (1,), row)))
        for row in range(0, 512, KEYS):
            held_row = flip_low * 512 + row
            last_pieces.append((flip_low, 2, row, (0, (), held_row), (1, (), held_row)))

    state = attend(KEYS, pieces, arrays, place, ids_own, ids_low, encoder_segments, blocks)
    arrays = [across_keys, across_values]
    contexts = attend(
        KEYS, last_pieces, arrays, place, ids_own, ids_low, encoder_segments, blocks, state
    )

    contexts = (contexts[0],) + tuple(
        send(context, pairs) for context, pairs in zip(contexts[1:], (Y_FAR, Y_LOW, Y_CUT))
    )
    summed = []
    for part in range(2):
        both = outputs(place, contexts, w_own, far_rows, part, 2)
        summed.append(both[:128].astype(F32) + send(both[128:], CORE).astype(F32))
    return (jnp.concatenate(summed, axis=1) + local_rows.astype(F32)).astype(BF16)[None]


def solution(mesh):
    in_specs = (
        P("section", ("seq", "mp"), None),
        P(None, "seq", ("section", "mp")),
        P("section", None),
        P("section", None, "mp"),
        P("section", None, "mp"),
        P("section", None, "mp"),
        P("section", "mp", None),
        P("section", "seq"),
        P("section", None),
    )
    out_specs = P("section", ("seq", "mp"), None)
    return jax.shard_map(
        per_device, mesh=mesh, in_specs=in_specs, out_specs=out_specs, check_vma=False
    )
```
